32 devices in a mesh: day: 16 (over z, x, core), pair: 2 (over y).
Axes of the slice: x: 2, y: 2, z: 4, core: 2. Of those that a mesh axis runs over, the one named last changes fastest.
Arguments:
- spectra: bfloat16 [64, 128, 1024], P('day', 'pair'), may hold values from -4 to 4
- pair_list: int32 [1024, 2], P('pair'), may hold values from 0 to 127, as said below
- mask: int32 [64, 128], P('day'), may hold values from 0 to 1
Outputs:
- linear_stack: float32 [401, 1024], P(None, ('pair', 'day'))
- weighted_stack: float32 [401, 1024], P(None, ('pair', 'day'))
The draws below stay inside these ranges and needn't reach their ends.
Inputs may be any that keep to these rules, and one draw needn't show every extreme that they name: `pair_list`: the two stations of a pair differ.
All inputs are finite; a program needn't handle non-finite values.
Results may differ from the reference program's by a relative error of at most 0.0039.
Values may be sent and summed in bfloat16 or wider, within the bound.
A program may use at most 64 MiB of HBM per device.

```python
import math
import jax
import jax.numpy as jnp
from jax import lax

F = 512
MAXLAG = 200
STATIONS = 128
LAGS = 401
DAYS = 64
PAIRS = 1024


def draw_spectra(key, part):
    first_key, second_key = jax.random.split(jax.random.fold_in(key, 11))
    common = jax.random.normal(first_key, (STATIONS, 2 * F), jnp.float32)
    noise = jax.random.normal(second_key, (DAYS, STATIONS, 2 * F), jnp.float32)
    whole = 0.8 * common[None] + 0.6 * noise
    return jnp.clip(whole, -4.0, 4.0).astype(jnp.bfloat16)


def draw_pair_list(key, part):
    first_key, second_key = jax.random.split(jax.random.fold_in(key, 23))
    first = jax.random.randint(first_key, (PAIRS,), 0, STATIONS, jnp.int32)
    offset = jax.random.randint(second_key, (PAIRS,), 1, STATIONS, jnp.int32)
    second = jnp.mod(first + offset, STATIONS)
    first = first.at[0].set(0)
    second = second.at[0].set(STATIONS - 1)
    return jnp.stack([first, second], 1).astype(jnp.int32)


def draw_mask(key, part):
    draws = jax.random.randint(jax.random.fold_in(key, 37), (DAYS, STATIONS), 0, 1000, jnp.int32)
    day_index = jnp.arange(DAYS, dtype=jnp.int32)
    limit = 300 + 600 * day_index // max(DAYS - 1, 1)
    live = (draws < limit[:, None]).astype(jnp.int32)
    return jnp.where(day_index[:, None] == 0, 1, live).astype(jnp.int32)


def setup_inputs(seed: int = 0) -> dict:
    splits = jax.random.split(jax.random.key(seed), 4)
    spectra = draw_spectra(jax.random.fold_in(splits[3], 71), 0)
    pair_list = draw_pair_list(jax.random.fold_in(splits[3], 71), 0)
    mask = draw_mask(jax.random.fold_in(splits[3], 71), 0)
    return dict(spectra=spectra, pair_list=pair_list, mask=mask)


def lag_table():
    lag = jnp.arange(LAGS, dtype=jnp.int32) - MAXLAG
    freq = jnp.arange(F, dtype=jnp.int32)
    phase = jnp.mod(lag[:, None] * freq[None, :], 2 * F).astype(jnp.float32) * (math.pi / F)
    scale = 1.0 / math.sqrt(F)
    cosine = jnp.cos(phase) * scale
    sine = jnp.sin(phase) * scale
    upper = jnp.concatenate([cosine, -sine], 1)
    lower = jnp.concatenate([sine, cosine], 1)
    return jnp.concatenate([upper, lower], 0).astype(jnp.bfloat16)

def reference(spectra, pair_list, mask):
    table = lag_table()
    first = pair_list[:, 0].astype(jnp.int32)
    second = pair_list[:, 1].astype(jnp.int32)
    mask_float = mask.astype(jnp.float32)
    weights = jnp.take(mask_float, first, axis=1) * jnp.take(mask_float, second, axis=1)

    def one_day(carry, inputs):
        day_spec, weight = inputs
        left = jnp.take(day_spec, first, axis=0).astype(jnp.float32)
        right = jnp.take(day_spec, second, axis=0).astype(jnp.float32)
        left_re, left_im = (left[:, :F], left[:, F:])
        right_re, right_im = (right[:, :F], right[:, F:])
        cross_re = left_re * right_re + left_im * right_im
        cross_im = left_im * right_re - left_re * right_im
        cross = jnp.concatenate([cross_re, cross_im], 1).astype(jnp.bfloat16)
        analytic = lax.dot_general(table, cross, (((1,), (1,)), ((), ())), preferred_element_type=jnp.float32)
        trace = analytic[:LAGS]
        hilbert = analytic[LAGS:]
        amplitude = jnp.sqrt(trace * trace + hilbert * hilbert)
        inverse = 1.0 / jnp.maximum(amplitude, 0.5)
        lin_sum, real_sum, imag_sum = carry
        lin_sum = lin_sum + weight[None, :] * trace
        real_sum = real_sum + weight[None, :] * (trace * inverse)
        imag_sum = imag_sum + weight[None, :] * (hilbert * inverse)
        return ((lin_sum, real_sum, imag_sum), None)
    zeros = jnp.zeros((LAGS, pair_list.shape[0]), jnp.float32)
    (lin_sum, real_sum, imag_sum), _ = lax.scan(one_day, (zeros, zeros, zeros), (spectra, weights))
    count = lax.optimization_barrier(jnp.sum(weights, 0))[None, :]
    linear_stack = lin_sum / count
    weighted_stack = linear_stack * (real_sum * real_sum + imag_sum * imag_sum) / (count * count)
    return (linear_stack, weighted_stack)
```

```python
import functools
import math

import jax
import jax.numpy as jnp
import ml_dtypes
import numpy as np
from jax import lax
from jax.experimental import pallas as pl
from jax.experimental.pallas import tpu as pltpu
from jax.sharding import PartitionSpec as P

F = 512
MAXLAG = 200
LAGS = 401
LANES = 512
FULL = 384
PACKED = 1280
MESH = pl.DeviceIdType.MESH


def lag_table():
    lag = np.arange(LAGS) - MAXLAG
    freq = np.arange(F)
    phase = np.mod(lag[:, None] * freq[None, :], 2 * F) * (math.pi / F)
    cosine = np.cos(phase) / math.sqrt(F)
    sine = np.sin(phase) / math.sqrt(F)
    table = np.zeros((2 * F, 2 * LANES), np.float32)
    table[:F, :LAGS] = cosine.T
    table[F:, :LAGS] = -sine.T
    table[:F, LANES : LANES + LAGS] = sine.T
    table[F:, LANES : LANES + LAGS] = cosine.T
    return table.astype(ml_dtypes.bfloat16)


def streams_of(steps):
    straight = list(range(steps))
    turned = [0] + straight[2:] + [1] if steps > 2 else straight
    half = PACKED // 2
    return [(0, half, straight), (half, half, turned)]


def kernel(
    groups, halves, spectra, pairs, mask, table, lin_out, wgt_out,
    spec_all, table_v, pick, acc, tail, work, outbox, inbox,
    load_sem, gsend, grecv, rsend, rrecv,
):
    days, local, _ = spectra.shape
    rows = acc.shape[0]
    own = rows // groups
    steps = groups.bit_length() - 1
    streams = streams_of(steps)
    me = lax.axis_index("day")
    side = lax.axis_index("pair")

    def partner(bit):
        size = 1 << bit
        mine = lax.rem(lax.div(me, size), 2)
        return mine, me + (1 - 2 * mine) * size

    mine_rows = pl.ds(pl.multiple_of(side * local, local), local)
    loads = [
        pltpu.make_async_copy(spectra, spec_all.at[:, mine_rows, :], load_sem.at[0]),
        pltpu.make_async_copy(table, table_v, load_sem.at[1]),
    ]
    for copy in loads:
        copy.start()

    barrier = pltpu.get_barrier_semaphore()
    for off in range(1, halves):
        pl.semaphore_signal(
            barrier, inc=1, device_id=(me, lax.rem(side + off, halves)), device_id_type=MESH
        )
    for bit in range(steps):
        pl.semaphore_signal(barrier, inc=1, device_id=(partner(bit)[1], side), device_id_type=MESH)
    pl.semaphore_wait(barrier, halves - 1 + steps)

    def gather(day, off):
        return pltpu.make_async_remote_copy(
            src_ref=spectra.at[day],
            dst_ref=spec_all.at[day, mine_rows, :],
            send_sem=gsend.at[day, off - 1],
            recv_sem=grecv.at[day, off - 1],
            device_id=(me, lax.rem(side + off, halves)),
            device_id_type=MESH,
        )

    for day in range(days):
        for off in range(1, halves):
            gather(day, off).start()

    stations = local * halves
    row = lax.broadcasted_iota(jnp.int32, (stations, rows), 0)
    for end in range(2):
        hot = (pairs[end : end + 1, :] == row).astype(jnp.float32)
        pick[end] = hot.T
    acc[...] = jnp.zeros_like(acc)
    tail[...] = jnp.zeros_like(tail)
    live = mask[...].astype(jnp.float32)
    seen = [
        lax.dot_general(
            pick[end], live, (((1,), (1,)), ((), ())), preferred_element_type=jnp.float32
        )
        for end in range(2)
    ]
    count = jnp.sum(seen[0] * seen[1], 1, keepdims=True)
    lane = lax.broadcasted_iota(jnp.int32, (rows, 128), 1)
    tail[0] = jnp.where(lane == 96, count, 0.0)
    for copy in loads:
        copy.wait()

    block = min(rows, 256)

    def one_day(day, carry):
        for off in range(1, halves):
            gather(day, off).wait()
        today = mask[pl.ds(day, 1), :].astype(jnp.float32)
        spec = spec_all[day]
        for start in range(0, rows, block):
            here = pl.ds(start, block)
            left, right = (
                jnp.dot(
                    (pick[end, here] * today).astype(jnp.bfloat16),
                    spec,
                    preferred_element_type=jnp.float32,
                )
                for end in range(2)
            )
            left_re, left_im = left[:, :F], left[:, F:]
            right_re, right_im = right[:, :F], right[:, F:]
            cross = jnp.concatenate(
                [
                    (left_re * right_re + left_im * right_im).astype(jnp.bfloat16),
                    (left_im * right_re - left_re * right_im).astype(jnp.bfloat16),
                ],
                1,
            )
            analytic = jnp.dot(cross, table_v[...], preferred_element_type=jnp.float32)
            trace, hilbert = analytic[:, :LANES], analytic[:, LANES:]
            inverse = lax.rsqrt(jnp.maximum(trace * trace + hilbert * hilbert, 0.25))
            for n, value in enumerate((trace, trace * inverse, hilbert * inverse)):
                acc[here, n * FULL : (n + 1) * FULL] += value[:, :FULL]
                tail[n, here, :] += value[:, FULL:]
        return carry

    lax.fori_loop(0, days, one_day, 0)
    acc[:, 3 * FULL :] = tail[0] + pltpu.roll(tail[1], 32, 1) + pltpu.roll(tail[2], 64, 1)

    def exchange(s, k):
        blocks = groups >> (k + 1)
        base = groups - (groups >> k)
        return pltpu.make_async_remote_copy(
            src_ref=outbox.at[s, pl.ds(base, blocks)],
            dst_ref=inbox.at[s, pl.ds(base, blocks)],
            send_sem=rsend.at[s, k],
            recv_sem=rrecv.at[s, k],
            device_id=(partner(streams[s][2][k])[1], side),
            device_id_type=MESH,
        )

    def first_rows(s, i, bit):
        order = streams[s][2]
        natural = sum(((i >> (steps - 1 - n)) & 1) << order[n] for n in range(1, steps))
        return pl.ds(pl.multiple_of((natural + bit) * own, own), own)

    for k in range(steps + 1):
        for s, (lane0, width, order) in enumerate(streams):
            lanes = pl.ds(lane0, width)
            if k:
                mine, _ = partner(order[k - 1])
                blocks = groups >> k
                base = groups - (groups >> (k - 1))
                before = groups - (groups >> (k - 2)) if k > 1 else 0
                exchange(s, k - 1).wait_recv()
                for i in range(blocks):
                    if k == 1:
                        kept = acc[first_rows(s, i, mine), lanes]
                    else:
                        kept = work[s, before + mine * blocks + i]
                    work[s, base + i] = kept + inbox[s, base + i].astype(jnp.float32)
            if k < steps:
                mine, _ = partner(order[k])
                blocks = groups >> (k + 1)
                base = groups - (groups >> k)
                before = groups - (groups >> (k - 1)) if k else 0
                for i in range(blocks):
                    if k == 0:
                        sent = acc[first_rows(s, i, 1 - mine), lanes]
                    else:
                        sent = work[s, before + (1 - mine) * blocks + i]
                    outbox[s, base + i] = sent.astype(jnp.bfloat16)
                exchange(s, k).start()
    for s in range(len(streams)):
        for k in range(steps):
            exchange(s, k).wait_send()

    last = groups - 2
    whole = jnp.concatenate([work[s, last] for s in range(len(streams))], 1)
    rest = whole[:, 3 * FULL :]
    total = rest[:, 96:97]
    sums = [
        jnp.concatenate(
            [whole[:, n * FULL : (n + 1) * FULL], pltpu.roll(rest, (128 - 32 * n) % 128, 1)], 1
        )
        for n in range(3)
    ]
    linear = sums[0] / total
    lin_out[...] = linear
    wgt_out[...] = linear * (sums[1] * sums[1] + sums[2] * sums[2]) / (total * total)


def per_device(spectra, pair_list, mask, *, groups, halves):
    days, local, width = spectra.shape
    rows = pair_list.shape[0]
    own = rows // groups
    steps = groups.bit_length() - 1
    streams = len(streams_of(steps))
    half = PACKED // streams
    hbm = pl.BlockSpec(memory_space=pl.ANY)
    vmem = pl.BlockSpec(memory_space=pltpu.VMEM)
    lin, wgt = pl.pallas_call(
        functools.partial(kernel, groups, halves),
        out_shape=[jax.ShapeDtypeStruct((own, LANES), jnp.float32)] * 2,
        in_specs=[hbm, vmem, vmem, hbm],
        out_specs=[vmem, vmem],
        scratch_shapes=[
            pltpu.VMEM((days, local * halves, width), jnp.bfloat16),
            pltpu.VMEM((2 * F, 2 * LANES), jnp.bfloat16),
            pltpu.VMEM((2, rows, local * halves), jnp.float32),
            pltpu.VMEM((rows, PACKED), jnp.float32),
            pltpu.VMEM((3, rows, 128), jnp.float32),
            pltpu.VMEM((streams, groups, own, half), jnp.float32),
            pltpu.VMEM((streams, groups, own, half), jnp.bfloat16),
            pltpu.VMEM((streams, groups, own, half), jnp.bfloat16),
            pltpu.SemaphoreType.DMA((2,)),
            pltpu.SemaphoreType.DMA((days, halves - 1)),
            pltpu.SemaphoreType.DMA((days, halves - 1)),
            pltpu.SemaphoreType.DMA((streams, steps)),
            pltpu.SemaphoreType.DMA((streams, steps)),
        ],
        compiler_params=pltpu.CompilerParams(
            collective_id=0, has_side_effects=True, vmem_limit_bytes=48 * 1024 * 1024
        ),
    )(spectra, pair_list.T, mask, jnp.asarray(lag_table()))
    return lin[:, :LAGS].T, wgt[:, :LAGS].T


def solution(mesh):
    in_specs = (P("day", "pair", None), P("pair", None), P("day", None))
    out_specs = (P(None, ("pair", "day")), P(None, ("pair", "day")))
    return jax.shard_map(
        functools.partial(per_device, groups=mesh.shape["day"], halves=mesh.shape["pair"]),
        mesh=mesh,
        in_specs=in_specs,
        out_specs=out_specs,
        check_vma=False,
    )
```

```python
import functools
import math

import jax
import jax.numpy as jnp
import ml_dtypes
import numpy as np
from jax import lax
from jax.experimental import pallas as pl
from jax.experimental.pallas import tpu as pltpu
from jax.sharding import PartitionSpec as P

F = 512
MAXLAG = 200
LAGS = 401
LANES = 512
FULL = 384
PACKED = 1280
MESH = pl.DeviceIdType.MESH
VMEM_LIMIT = 64 * 1024 * 1024


def lag_table():
    lag = np.arange(LAGS) - MAXLAG
    freq = np.arange(F)
    phase = np.mod(lag[:, None] * freq[None, :], 2 * F) * (math.pi / F)
    cosine = np.cos(phase) / math.sqrt(F)
    sine = np.sin(phase) / math.sqrt(F)
    table = np.zeros((2 * F, 2 * LANES), np.float32)
    table[:F, :LAGS] = cosine.T
    table[F:, :LAGS] = -sine.T
    table[:F, LANES : LANES + LAGS] = sine.T
    table[F:, LANES : LANES + LAGS] = cosine.T
    return table.astype(ml_dtypes.bfloat16)


def parts_of(own):
    return 2 if own % 32 == 0 else 1


def streams_of(steps, parts):
    straight = list(range(steps))
    turned = [0] + straight[2:] + [1] if steps > 2 else straight
    half = PACKED // 2
    return [(p, n * half, half, order) for p in range(parts) for n, order in enumerate((straight, turned))]


def kernel(
    groups, halves, spectra, pairs_hbm, mask_hbm, table, lin_out, wgt_out,
    spec_all, table_v, pairs, mask, pick, acc, tail, work, outbox, inbox,
    load_sem, gsend, grecv, rsend, rrecv,
):
    days, local, _ = spectra.shape
    parts, rows, _ = acc.shape
    own = rows // groups
    steps = groups.bit_length() - 1
    streams = streams_of(steps, parts)
    me = lax.axis_index("day")
    side = lax.axis_index("pair")

    def partner(bit):
        size = 1 << bit
        mine = lax.rem(lax.div(me, size), 2)
        return mine, me + (1 - 2 * mine) * size

    mine_rows = pl.ds(pl.multiple_of(side * local, local), local)
    loads = [
        pltpu.make_async_copy(pairs_hbm, pairs, load_sem.at[0]),
        pltpu.make_async_copy(mask_hbm, mask, load_sem.at[1]),
        pltpu.make_async_copy(spectra, spec_all.at[:, mine_rows, :], load_sem.at[2]),
        pltpu.make_async_copy(table, table_v, load_sem.at[3]),
    ]
    for copy in loads:
        copy.start()

    barrier = pltpu.get_barrier_semaphore()
    for off in range(1, halves):
        pl.semaphore_signal(
            barrier, inc=1, device_id=(me, lax.rem(side + off, halves)), device_id_type=MESH
        )
    for bit in range(steps):
        pl.semaphore_signal(barrier, inc=1, device_id=(partner(bit)[1], side), device_id_type=MESH)
    pl.semaphore_wait(barrier, halves - 1 + steps)

    def gather(day, off):
        return pltpu.make_async_remote_copy(
            src_ref=spectra.at[day],
            dst_ref=spec_all.at[day, mine_rows, :],
            send_sem=gsend.at[day, off - 1],
            recv_sem=grecv.at[day, off - 1],
            device_id=(me, lax.rem(side + off, halves)),
            device_id_type=MESH,
        )

    for day in range(days):
        for off in range(1, halves):
            gather(day, off).start()

    stations = local * halves
    loads[0].wait()
    loads[1].wait()
    row = lax.broadcasted_iota(jnp.int32, (stations, rows * parts), 0)
    for end in range(2):
        hot = (pairs[end : end + 1, :] == row).astype(jnp.float32).T
        hot = hot.reshape(groups, parts, own, stations)
        for part in range(parts):
            pick[end, part] = hot[:, part].reshape(rows, stations)
    acc[...] = jnp.zeros_like(acc)
    tail[...] = jnp.zeros_like(tail)
    live = mask[...].astype(jnp.float32)
    lane = lax.broadcasted_iota(jnp.int32, (rows, 128), 1)
    for part in range(parts):
        seen = [
            lax.dot_general(
                pick[end, part], live, (((1,), (1,)), ((), ())), preferred_element_type=jnp.float32
            )
            for end in range(2)
        ]
        count = jnp.sum(seen[0] * seen[1], 1, keepdims=True)
        tail[0, part] = jnp.where(lane == 96, count, 0.0)
    loads[2].wait()
    loads[3].wait()

    block = min(rows, 256)

    def arrive(day):
        for off in range(1, halves):
            gather(day, off).wait()

    def correlate(day, part):
        today = mask[pl.ds(day, 1), :].astype(jnp.float32)
        spec = spec_all[day]
        for start in range(0, rows, block):
            here = pl.ds(start, block)
            left, right = (
                jnp.dot(
                    (pick[end, part, here] * today).astype(jnp.bfloat16),
                    spec,
                    preferred_element_type=jnp.float32,
                )
                for end in range(2)
            )
            left_re, left_im = left[:, :F], left[:, F:]
            right_re, right_im = right[:, :F], right[:, F:]
            cross = jnp.concatenate(
                [
                    (left_re * right_re + left_im * right_im).astype(jnp.bfloat16),
                    (left_im * right_re - left_re * right_im).astype(jnp.bfloat16),
                ],
                1,
            )
            analytic = jnp.dot(cross, table_v[...], preferred_element_type=jnp.float32)
            trace, hilbert = analytic[:, :LANES], analytic[:, LANES:]
            inverse = lax.rsqrt(jnp.maximum(trace * trace + hilbert * hilbert, 0.25))
            for n, value in enumerate((trace, trace * inverse, hilbert * inverse)):
                acc[part, here, n * FULL : (n + 1) * FULL] += value[:, :FULL]
                tail[n, part, here] += value[:, FULL:]

    def exchange(s, k):
        blocks = groups >> (k + 1)
        base = groups - (groups >> k)
        return pltpu.make_async_remote_copy(
            src_ref=outbox.at[s, pl.ds(base, blocks)],
            dst_ref=inbox.at[s, pl.ds(base, blocks)],
            send_sem=rsend.at[s, k],
            recv_sem=rrecv.at[s, k],
            device_id=(partner(streams[s][3][k])[1], side),
            device_id_type=MESH,
        )

    def first_rows(order, i, bit):
        natural = sum(((i >> (steps - 1 - n)) & 1) << order[n] for n in range(1, steps))
        return pl.ds(pl.multiple_of((natural + bit) * own, own), own)

    def send(s, k):
        part, lane0, width, order = streams[s]
        theirs = 1 - partner(order[k])[0]
        blocks = groups >> (k + 1)
        base = groups - (groups >> k)
        before = groups - (groups >> (k - 1)) if k else 0
        for i in range(blocks):
            if k == 0:
                sent = acc[part, first_rows(order, i, theirs), pl.ds(lane0, width)]
            else:
                sent = work[s, before + theirs * blocks + i]
            outbox[s, base + i] = sent.astype(jnp.bfloat16)
        exchange(s, k).start()

    def receive(s, k):
        part, lane0, width, order = streams[s]
        mine = partner(order[k])[0]
        blocks = groups >> (k + 1)
        base = groups - (groups >> k)
        before = groups - (groups >> (k - 1)) if k else 0
        exchange(s, k).wait_recv()
        for i in range(blocks):
            if k == 0:
                kept = acc[part, first_rows(order, i, mine), pl.ds(lane0, width)]
            else:
                kept = work[s, before + mine * blocks + i]
            work[s, base + i] = kept + inbox[s, base + i].astype(jnp.float32)

    def one_day(day, carry):
        arrive(day)
        for part in range(parts):
            correlate(day, part)
        return carry

    lax.fori_loop(0, days - 1, one_day, 0)
    arrive(days - 1)
    for part in range(parts):
        correlate(days - 1, part)
        acc[part, :, 3 * FULL :] = (
            tail[0, part] + pltpu.roll(tail[1, part], 32, 1) + pltpu.roll(tail[2, part], 64, 1)
        )
        for s in range(len(streams)):
            if streams[s][0] == part:
                send(s, 0)
    for k in range(steps):
        for s in range(len(streams)):
            receive(s, k)
            if k + 1 < steps:
                send(s, k + 1)

    last = groups - 2
    for part in range(parts):
        whole = jnp.concatenate([work[s, last] for s in range(len(streams)) if streams[s][0] == part], 1)
        rest = whole[:, 3 * FULL :]
        total = rest[:, 96:97]
        sums = [
            jnp.concatenate(
                [whole[:, n * FULL : (n + 1) * FULL], pltpu.roll(rest, (128 - 32 * n) % 128, 1)], 1
            )
            for n in range(3)
        ]
        linear = sums[0] / total
        here = pl.ds(part * own, own)
        lin_out[here] = linear
        wgt_out[here] = linear * (sums[1] * sums[1] + sums[2] * sums[2]) / (total * total)
    for s in range(len(streams)):
        for k in range(steps):
            exchange(s, k).wait_send()


def per_device(spectra, pair_list, mask, *, groups, halves):
    days, local, width = spectra.shape
    rows = pair_list.shape[0]
    parts = parts_of(rows // groups)
    own = rows // groups // parts
    steps = groups.bit_length() - 1
    streams = len(streams_of(steps, parts))
    half = PACKED // 2
    hbm = pl.BlockSpec(memory_space=pl.ANY)
    vmem = pl.BlockSpec(memory_space=pltpu.VMEM)
    lin, wgt = pl.pallas_call(
        functools.partial(kernel, groups, halves),
        out_shape=[jax.ShapeDtypeStruct((own * parts, LANES), jnp.float32)] * 2,
        in_specs=[hbm] * 4,
        out_specs=[vmem, vmem],
        scratch_shapes=[
            pltpu.VMEM((days, local * halves, width), jnp.bfloat16),
            pltpu.VMEM((2 * F, 2 * LANES), jnp.bfloat16),
            pltpu.VMEM((2, rows), jnp.int32),
            pltpu.VMEM(mask.shape, jnp.int32),
            pltpu.VMEM((2, parts, rows // parts, local * halves), jnp.float32),
            pltpu.VMEM((parts, rows // parts, PACKED), jnp.float32),
            pltpu.VMEM((3, parts, rows // parts, 128), jnp.float32),
            pltpu.VMEM((streams, groups, own, half), jnp.float32),
            pltpu.VMEM((streams, groups, own, half), jnp.bfloat16),
            pltpu.VMEM((streams, groups, own, half), jnp.bfloat16),
            pltpu.SemaphoreType.DMA((4,)),
            pltpu.SemaphoreType.DMA((days, halves - 1)),
            pltpu.SemaphoreType.DMA((days, halves - 1)),
            pltpu.SemaphoreType.DMA((streams, steps)),
            pltpu.SemaphoreType.DMA((streams, steps)),
        ],
        compiler_params=pltpu.CompilerParams(
            collective_id=0, has_side_effects=True, vmem_limit_bytes=VMEM_LIMIT
        ),
    )(spectra, pair_list.T, mask, jnp.asarray(lag_table()))
    return lin[:, :LAGS].T, wgt[:, :LAGS].T


def solution(mesh):
    in_specs = (P("day", "pair", None), P("pair", None), P("day", None))
    out_specs = (P(None, ("pair", "day")), P(None, ("pair", "day")))
    return jax.shard_map(
        functools.partial(per_device, groups=mesh.shape["day"], halves=mesh.shape["pair"]),
        mesh=mesh,
        in_specs=in_specs,
        out_specs=out_specs,
        check_vma=False,
    )
```

```python
import functools
import math

import jax
import jax.numpy as jnp
import ml_dtypes
import numpy as np
from jax import lax
from jax.experimental import pallas as pl
from jax.experimental.pallas import tpu as pltpu
from jax.sharding import PartitionSpec as P

F = 512
MAXLAG = 200
LAGS = 401
LANES = 512
FULL = 384
PACKED = 1280
MESH = pl.DeviceIdType.MESH
VMEM_LIMIT = 40 * 1024 * 1024


def lag_table():
    lag = np.arange(LAGS) - MAXLAG
    freq = np.arange(F)
    phase = np.mod(lag[:, None] * freq[None, :], 2 * F) * (math.pi / F)
    cosine = np.cos(phase) / math.sqrt(F)
    sine = np.sin(phase) / math.sqrt(F)
    table = np.zeros((2 * F, 2 * LANES), np.float32)
    table[:F, :LAGS] = cosine.T
    table[F:, :LAGS] = -sine.T
    table[:F, LANES : LANES + LAGS] = sine.T
    table[F:, LANES : LANES + LAGS] = cosine.T
    return table.astype(ml_dtypes.bfloat16)


def parts_of(own):
    return 2 if own % 32 == 0 else 1


def parts_of(own):
    return 2 if own % 32 == 0 else 1


def streams_of(steps, parts):
    straight = list(range(steps))
    half = PACKED // 2
    return [
        (p, n * half, half, order)
        for p in range(parts)
        for n, order in enumerate((straight, straight[1:] + straight[:1]))
    ]


def kernel(
    chips, halves, spectra, pairs_hbm, mask_hbm, table, lin_out, wgt_out,
    spec_all, table_v, pairs, mask, hot, pick, acc, tail, work, outbox, inbox,
    load_sem, gsend, grecv, fsend, frecv, dsend, drecv, rsend, rrecv,
):
    days, local, _ = spectra.shape
    rows = acc.shape[0]
    steps = chips.bit_length() - 1
    parts = parts_of(rows // chips)
    per_part = rows // parts
    own = per_part // chips
    streams = streams_of(steps, parts)
    me = lax.axis_index("day")
    side = lax.axis_index("pair")
    core = lax.rem(me, 2)
    sibling = me + 1 - 2 * core

    def partner(bit):
        size = 2 << bit
        mine = lax.rem(lax.div(me, size), 2)
        return mine, me + (1 - 2 * mine) * size

    def stations_of(where):
        return pl.ds(pl.multiple_of(where * local, local), local)

    mine_rows = stations_of(side)
    loads = [
        pltpu.make_async_copy(pairs_hbm, pairs, load_sem.at[0]),
        pltpu.make_async_copy(mask_hbm, mask.at[core], load_sem.at[1]),
        pltpu.make_async_copy(spectra, spec_all.at[core, :, mine_rows, :], load_sem.at[2]),
        pltpu.make_async_copy(table, table_v, load_sem.at[3]),
    ]
    for copy in loads:
        copy.start()

    barrier = pltpu.get_barrier_semaphore()
    for off in range(1, halves):
        pl.semaphore_signal(
            barrier, inc=1, device_id=(me, lax.rem(side + off, halves)), device_id_type=MESH
        )
    pl.semaphore_signal(barrier, inc=1, device_id=(sibling, side), device_id_type=MESH)
    for bit in range(steps):
        pl.semaphore_signal(barrier, inc=1, device_id=(partner(bit)[1], side), device_id_type=MESH)
    pl.semaphore_wait(barrier, halves + steps)

    def gather(day, off):
        return pltpu.make_async_remote_copy(
            src_ref=spectra.at[day],
            dst_ref=spec_all.at[core, day, mine_rows, :],
            send_sem=gsend.at[day, off - 1],
            recv_sem=grecv.at[day, off - 1],
            device_id=(me, lax.rem(side + off, halves)),
            device_id_type=MESH,
        )

    def forward(day, off):
        here = spec_all.at[core, day, stations_of(lax.rem(side + halves - off, halves)), :]
        return pltpu.make_async_remote_copy(
            src_ref=here,
            dst_ref=here,
            send_sem=fsend.at[day, off - 1],
            recv_sem=frecv.at[day, off - 1],
            device_id=(sibling, side),
            device_id_type=MESH,
        )

    def direct(day):
        return pltpu.make_async_remote_copy(
            src_ref=spectra.at[day],
            dst_ref=spec_all.at[core, day, mine_rows, :],
            send_sem=dsend.at[day],
            recv_sem=drecv.at[day],
            device_id=(sibling, side),
            device_id_type=MESH,
        )

    mask_copy = pltpu.make_async_remote_copy(
        src_ref=mask_hbm,
        dst_ref=mask.at[core],
        send_sem=dsend.at[days],
        recv_sem=drecv.at[days],
        device_id=(sibling, side),
        device_id_type=MESH,
    )

    for day in range(days):
        for off in range(1, halves):
            gather(day, off).start()
        if day == 0:
            mask_copy.start()
        direct(day).start()

    stations = local * halves
    loads[0].wait()
    for end in range(2):
        row = lax.broadcasted_iota(jnp.int32, (stations, 2 * rows), 0)
        hot[...] = (pairs[end : end + 1, :] == row).astype(jnp.float32).T
        for part in range(parts):
            for chip in range(chips):
                first = (2 * chip + core) * (own * parts) + part * own
                pick[end, pl.ds(part * per_part + chip * own, own)] = hot[
                    pl.ds(pl.multiple_of(first, own), own)
                ]
    acc[...] = jnp.zeros_like(acc)
    tail[...] = jnp.zeros_like(tail)
    loads[1].wait()
    mask_copy.wait_recv()
    count = 0.0
    for owner in range(2):
        seen = [
            lax.dot_general(
                pick[end],
                mask[owner].astype(jnp.float32),
                (((1,), (1,)), ((), ())),
                preferred_element_type=jnp.float32,
            )
            for end in range(2)
        ]
        count += jnp.sum(seen[0] * seen[1], 1, keepdims=True)
    lane = lax.broadcasted_iota(jnp.int32, (rows, 128), 1)
    tail[0] = jnp.where(lane == 96, count, 0.0)
    loads[2].wait()
    loads[3].wait()

    def correlate(owner, day, start, size):
        today = mask[owner, pl.ds(day, 1), :].astype(jnp.float32)
        spec = spec_all[owner, day]
        here = pl.ds(start, size)
        left, right = (
            jnp.dot(
                (pick[end, here] * today).astype(jnp.bfloat16),
                spec,
                preferred_element_type=jnp.float32,
            )
            for end in range(2)
        )
        left_re, left_im = left[:, :F], left[:, F:]
        right_re, right_im = right[:, :F], right[:, F:]
        cross = jnp.concatenate(
            [
                (left_re * right_re + left_im * right_im).astype(jnp.bfloat16),
                (left_im * right_re - left_re * right_im).astype(jnp.bfloat16),
            ],
            1,
        )
        analytic = jnp.dot(cross, table_v[...], preferred_element_type=jnp.float32)
        trace, hilbert = analytic[:, :LANES], analytic[:, LANES:]
        inverse = lax.rsqrt(jnp.maximum(trace * trace + hilbert * hilbert, 0.25))
        for n, value in enumerate((trace, trace * inverse, hilbert * inverse)):
            acc[here, n * FULL : (n + 1) * FULL] += value[:, :FULL]
            tail[n, here] += value[:, FULL:]

    def exchange(s, k):
        blocks = chips >> (k + 1)
        base = chips - (chips >> k)
        return pltpu.make_async_remote_copy(
            src_ref=outbox.at[s, pl.ds(base, blocks)],
            dst_ref=inbox.at[s, pl.ds(base, blocks)],
            send_sem=rsend.at[s, k],
            recv_sem=rrecv.at[s, k],
            device_id=(partner(streams[s][3][k])[1], side),
            device_id_type=MESH,
        )

    def first_rows(part, order, i, bit):
        natural = sum(((i >> (steps - 1 - n)) & 1) << order[n] for n in range(1, steps))
        first = part * per_part + (natural + bit * (1 << order[0])) * own
        return pl.ds(pl.multiple_of(first, own), own)

    def send(s, k):
        part, lane0, width, order = streams[s]
        theirs = 1 - partner(order[k])[0]
        blocks = chips >> (k + 1)
        base = chips - (chips >> k)
        before = chips - (chips >> (k - 1)) if k else 0
        for i in range(blocks):
            if k == 0:
                sent = acc[first_rows(part, order, i, theirs), pl.ds(lane0, width)]
            else:
                sent = work[s, before + theirs * blocks + i]
            outbox[s, base + i] = sent.astype(jnp.bfloat16)
        exchange(s, k).start()

    def receive(s, k):
        part, lane0, width, order = streams[s]
        mine = partner(order[k])[0]
        blocks = chips >> (k + 1)
        base = chips - (chips >> k)
        before = chips - (chips >> (k - 1)) if k else 0
        exchange(s, k).wait_recv()
        for i in range(blocks):
            if k == 0:
                kept = acc[first_rows(part, order, i, mine), pl.ds(lane0, width)]
            else:
                kept = work[s, before + mine * blocks + i]
            work[s, base + i] = kept + inbox[s, base + i].astype(jnp.float32)

    def own_day(day):
        for off in range(1, halves):
            gather(day, off).wait_recv()
            forward(day, off).start()
        correlate(core, day, 0, rows)
        direct(day).wait_recv()
        for off in range(1, halves):
            forward(day, off).wait_recv()

    def one_day(day, carry):
        own_day(day)
        correlate(1 - core, day, 0, rows)
        return carry

    lax.fori_loop(0, days - 1, one_day, 0)
    own_day(days - 1)
    for part in range(parts):
        here = pl.ds(part * per_part, per_part)
        correlate(1 - core, days - 1, part * per_part, per_part)
        acc[here, 3 * FULL :] = (
            tail[0, here] + pltpu.roll(tail[1, here], 32, 1) + pltpu.roll(tail[2, here], 64, 1)
        )
        for s in range(len(streams)):
            if streams[s][0] == part:
                send(s, 0)
    for k in range(steps):
        for s in range(len(streams)):
            receive(s, k)
            if k + 1 < steps:
                send(s, k + 1)

    last = chips - 2
    for part in range(parts):
        whole = jnp.concatenate(
            [work[s, last] for s in range(len(streams)) if streams[s][0] == part], 1
        )
        rest = whole[:, 3 * FULL :]
        total = rest[:, 96:97]
        sums = [
            jnp.concatenate(
                [whole[:, n * FULL : (n + 1) * FULL], pltpu.roll(rest, (128 - 32 * n) % 128, 1)], 1
            )
            for n in range(3)
        ]
        linear = sums[0] / total
        here = pl.ds(part * own, own)
        lin_out[here] = linear
        wgt_out[here] = linear * (sums[1] * sums[1] + sums[2] * sums[2]) / (total * total)
    mask_copy.wait_send()
    for day in range(days):
        direct(day).wait_send()
        for off in range(1, halves):
            gather(day, off).wait_send()
            forward(day, off).wait_send()
    for s in range(len(streams)):
        for k in range(steps):
            exchange(s, k).wait_send()


def per_device(spectra, pair_list, mask, *, groups, halves):
    days, local, width = spectra.shape
    chips = groups // 2
    rows = pair_list.shape[0] // 2
    parts = parts_of(rows // chips)
    own = rows // chips // parts
    steps = chips.bit_length() - 1
    streams = len(streams_of(steps, parts))
    half = PACKED // 2
    stations = local * halves
    operands = (spectra, pair_list.T, mask, jnp.asarray(lag_table()))
    hbm = pl.BlockSpec(memory_space=pltpu.HBM)
    vmem = pl.BlockSpec(memory_space=pltpu.VMEM)
    lin, wgt = pl.pallas_call(
        functools.partial(kernel, chips, halves),
        out_shape=[jax.ShapeDtypeStruct((own * parts, LANES), jnp.float32)] * 2,
        in_specs=[hbm] * 4,
        out_specs=[vmem, vmem],
        scratch_shapes=[
            pltpu.VMEM((2, days, stations, width), jnp.bfloat16),
            pltpu.VMEM((2 * F, 2 * LANES), jnp.bfloat16),
            pltpu.VMEM((2, 2 * rows), jnp.int32),
            pltpu.VMEM((2, *mask.shape), jnp.int32),
            pltpu.VMEM((2 * rows, stations), jnp.float32),
            pltpu.VMEM((2, rows, stations), jnp.float32),
            pltpu.VMEM((rows, PACKED), jnp.float32),
            pltpu.VMEM((3, rows, 128), jnp.float32),
            pltpu.VMEM((streams, chips, own, half), jnp.float32),
            pltpu.VMEM((streams, chips, own, half), jnp.bfloat16),
            pltpu.VMEM((streams, chips, own, half), jnp.bfloat16),
            pltpu.SemaphoreType.DMA((4,)),
            pltpu.SemaphoreType.DMA((days, halves - 1)),
            pltpu.SemaphoreType.DMA((days, halves - 1)),
            pltpu.SemaphoreType.DMA((days, halves - 1)),
            pltpu.SemaphoreType.DMA((days, halves - 1)),
            pltpu.SemaphoreType.DMA((days + 1,)),
            pltpu.SemaphoreType.DMA((days + 1,)),
            pltpu.SemaphoreType.DMA((streams, steps)),
            pltpu.SemaphoreType.DMA((streams, steps)),
        ],
        compiler_params=pltpu.CompilerParams(
            collective_id=0, has_side_effects=True, vmem_limit_bytes=VMEM_LIMIT
        ),
    )(*[pltpu.with_memory_space_constraint(x, pltpu.HBM) for x in operands])
    return lin[:, :LAGS].T, wgt[:, :LAGS].T


def solution(mesh):
    in_specs = (P("day", "pair", None), P("pair", None), P("day", None))
    out_specs = (P(None, ("pair", "day")), P(None, ("pair", "day")))
    return jax.shard_map(
        functools.partial(per_device, groups=mesh.shape["day"], halves=mesh.shape["pair"]),
        mesh=mesh,
        in_specs=in_specs,
        out_specs=out_specs,
        check_vma=False,
    )
```

```python
import functools
import math

import jax
import jax.numpy as jnp
import ml_dtypes
import numpy as np
from jax import lax
from jax.experimental import pallas as pl
from jax.experimental.pallas import tpu as pltpu
from jax.sharding import PartitionSpec as P

F = 512
MAXLAG = 200
LAGS = 401
LANES = 512
WIDE = 256
PACKED = 1280
SHARES = (896, 384)
MESH = pl.DeviceIdType.MESH
VMEM_LIMIT = 40 * 1024 * 1024


def lag_table():
    lag = np.arange(MAXLAG + 1)
    freq = np.arange(F)
    phase = np.mod(lag[None, :] * freq[:, None], 2 * F) * (math.pi / F)
    table = np.zeros((F, 2 * WIDE), np.float32)
    table[:, : MAXLAG + 1] = np.cos(phase) / math.sqrt(F)
    table[:, WIDE : WIDE + MAXLAG + 1] = np.sin(phase) / math.sqrt(F)
    return table.astype(ml_dtypes.bfloat16)


def packed_rest(tail, count):
    lane = lax.broadcasted_iota(jnp.int32, count.shape, 1)
    tiles = [
        jnp.where(lane < 64, tail[2 * n], pltpu.roll(tail[2 * n + 1], 64, 1)) for n in range(3)
    ]
    ends = count
    for j in range(6):
        ends += pltpu.roll(jnp.where(lane >= 64, tail[j], 0.0), (16 * j + 64) % 128, 1)
    return jnp.concatenate(tiles + [ends], 1)


def unpacked(whole):
    tile = [whole[:, n * 128 : (n + 1) * 128] for n in range(PACKED // 128)]
    lane = lax.broadcasted_iota(jnp.int32, tile[0].shape, 1)
    sums = []
    for j in range(6):
        middle = tile[6 + j // 2] if j % 2 == 0 else pltpu.roll(tile[6 + j // 2], 64, 1)
        end = pltpu.roll(tile[9], (192 - 16 * j) % 128, 1)
        rest = jnp.where(lane < 64, middle, jnp.where(lane < 73, end, 0.0))
        sums.append(jnp.concatenate([tile[j], rest], 1))
    return sums, tile[9][:, 96:97]


def in_order(plus, minus, turn):
    rows = minus.shape[0]
    high = minus.astype(jnp.bfloat16)
    left = minus - high.astype(jnp.float32)
    middle = left.astype(jnp.bfloat16)
    low = (left - middle.astype(jnp.float32)).astype(jnp.bfloat16)
    terms = jnp.dot(
        jnp.concatenate([high, middle, low], 0), turn, preferred_element_type=jnp.float32
    )
    turned = terms[:rows] + terms[rows : 2 * rows] + terms[2 * rows :]
    near, far = (pltpu.roll(plus[:, n * 128 : (n + 1) * 128], 72, 1) for n in range(2))
    lane = lax.broadcasted_iota(jnp.int32, near.shape, 1)
    return jnp.concatenate(
        [
            turned[:, :128],
            jnp.where(lane < 72, turned[:, 128:], near),
            jnp.where(lane < 72, near, far),
            far,
        ],
        1,
    )


def parts_of(own):
    return 2 if own % 32 == 0 else 1


def parts_of(own):
    return 2 if own % 32 == 0 else 1


def streams_of(steps, parts):
    straight = list(range(steps))
    swapped = straight[1::-1] + straight[2:]
    return [
        (p, n, n * SHARES[0], SHARES[n], order)
        for p in range(parts)
        for n, order in enumerate((straight, swapped))
    ]


def kernel(
    chips, halves, spectra, pairs_hbm, mask_hbm, table, lin_out, wgt_out,
    spec_all, table_v, pairs, mask, hot, pick, acc, tail, count, turn, *boxes_and_semaphores,
):
    work, outbox, inbox = (boxes_and_semaphores[2 * n : 2 * n + 2] for n in range(3))
    load_sem, gsend, grecv, fsend, frecv, dsend, drecv, rsend, rrecv = boxes_and_semaphores[6:]
    days, local, _ = spectra.shape
    rows = acc.shape[0]
    steps = chips.bit_length() - 1
    parts = parts_of(rows // chips)
    per_part = rows // parts
    own = per_part // chips
    streams = streams_of(steps, parts)
    me = lax.axis_index("day")
    side = lax.axis_index("pair")
    core = lax.rem(me, 2)
    sibling = me + 1 - 2 * core

    def partner(bit):
        size = 2 << bit
        mine = lax.rem(lax.div(me, size), 2)
        return mine, me + (1 - 2 * mine) * size

    def stations_of(where):
        return pl.ds(pl.multiple_of(where * local, local), local)

    mine_rows = stations_of(side)
    loads = [
        pltpu.make_async_copy(pairs_hbm, pairs, load_sem.at[0]),
        pltpu.make_async_copy(mask_hbm, mask.at[core], load_sem.at[1]),
        pltpu.make_async_copy(spectra, spec_all.at[core, :, mine_rows, :], load_sem.at[2]),
        pltpu.make_async_copy(table, table_v, load_sem.at[3]),
    ]
    for copy in loads:
        copy.start()

    barrier = pltpu.get_barrier_semaphore()
    for off in range(1, halves):
        pl.semaphore_signal(
            barrier, inc=1, device_id=(me, lax.rem(side + off, halves)), device_id_type=MESH
        )
    pl.semaphore_signal(barrier, inc=1, device_id=(sibling, side), device_id_type=MESH)
    for bit in range(steps):
        pl.semaphore_signal(barrier, inc=1, device_id=(partner(bit)[1], side), device_id_type=MESH)
    pl.semaphore_wait(barrier, halves + steps)

    def gather(day, off):
        return pltpu.make_async_remote_copy(
            src_ref=spectra.at[day],
            dst_ref=spec_all.at[core, day, mine_rows, :],
            send_sem=gsend.at[day, off - 1],
            recv_sem=grecv.at[day, off - 1],
            device_id=(me, lax.rem(side + off, halves)),
            device_id_type=MESH,
        )

    def forward(day, off):
        here = spec_all.at[core, day, stations_of(lax.rem(side + halves - off, halves)), :]
        return pltpu.make_async_remote_copy(
            src_ref=here,
            dst_ref=here,
            send_sem=fsend.at[day, off - 1],
            recv_sem=frecv.at[day, off - 1],
            device_id=(sibling, side),
            device_id_type=MESH,
        )

    def direct(day):
        return pltpu.make_async_remote_copy(
            src_ref=spectra.at[day],
            dst_ref=spec_all.at[core, day, mine_rows, :],
            send_sem=dsend.at[day],
            recv_sem=drecv.at[day],
            device_id=(sibling, side),
            device_id_type=MESH,
        )

    mask_copy = pltpu.make_async_remote_copy(
        src_ref=mask_hbm,
        dst_ref=mask.at[core],
        send_sem=dsend.at[days],
        recv_sem=drecv.at[days],
        device_id=(sibling, side),
        device_id_type=MESH,
    )

    for day in range(days):
        for off in range(1, halves):
            gather(day, off).start()
        if day == 0:
            mask_copy.start()
        direct(day).start()

    stations = local * halves
    loads[0].wait()
    for end in range(2):
        row = lax.broadcasted_iota(jnp.int32, (stations, 2 * rows), 0)
        hot[...] = (pairs[end : end + 1, :] == row).astype(jnp.float32).T
        for part in range(parts):
            for chip in range(chips):
                first = (2 * chip + core) * (own * parts) + part * own
                pick[end, pl.ds(part * per_part + chip * own, own)] = hot[
                    pl.ds(pl.multiple_of(first, own), own)
                ]
    acc[...] = jnp.zeros_like(acc)
    tail[...] = jnp.zeros_like(tail)
    loads[1].wait()
    mask_copy.wait_recv()
    alive = 0.0
    for owner in range(2):
        seen = [
            lax.dot_general(
                pick[end],
                mask[owner].astype(jnp.float32),
                (((1,), (1,)), ((), ())),
                preferred_element_type=jnp.float32,
            )
            for end in range(2)
        ]
        alive += jnp.sum(seen[0] * seen[1], 1, keepdims=True)
    lane = lax.broadcasted_iota(jnp.int32, (rows, 128), 1)
    count[...] = jnp.where(lane == 96, alive, 0.0)
    turn[...] = (
        (
            lax.broadcasted_iota(jnp.int32, (WIDE, WIDE), 0)
            + lax.broadcasted_iota(jnp.int32, (WIDE, WIDE), 1)
            == MAXLAG
        )
        .astype(jnp.float32)
        .astype(jnp.bfloat16)
    )
    loads[2].wait()
    loads[3].wait()

    def correlate(owner, day, start, size):
        today = mask[owner, pl.ds(day, 1), :].astype(jnp.float32)
        spec = spec_all[owner, day]
        here = pl.ds(start, size)
        both = jnp.dot(
            (pick[:, here] * today).astype(jnp.bfloat16).reshape(2 * size, spec.shape[0]),
            spec,
            preferred_element_type=jnp.float32,
        )
        left_re, left_im = both[:size, :F], both[:size, F:]
        right_re, right_im = both[size:, :F], both[size:, F:]
        cross = jnp.concatenate(
            [
                (left_re * right_re + left_im * right_im).astype(jnp.bfloat16),
                (left_im * right_re - left_re * right_im).astype(jnp.bfloat16),
            ],
            0,
        )
        waves = jnp.dot(cross, table_v[...], preferred_element_type=jnp.float32)
        re_cos, re_sin = waves[:size, :WIDE], waves[:size, WIDE:]
        im_cos, im_sin = waves[size:, :WIDE], waves[size:, WIDE:]
        for back in range(2):
            if back:
                trace, hilbert = re_cos + im_sin, im_cos - re_sin
            else:
                trace, hilbert = re_cos - im_sin, im_cos + re_sin
            inverse = lax.rsqrt(jnp.maximum(trace * trace + hilbert * hilbert, 0.25))
            for n, value in enumerate((trace, trace * inverse, hilbert * inverse)):
                j = 2 * n + back
                acc[here, j * 128 : (j + 1) * 128] += value[:, :128]
                tail[j, here] += value[:, 128:]

    def exchange(s, k):
        part, n, _, _, order = streams[s]
        blocks = chips >> (k + 1)
        base = chips - (chips >> k)
        return pltpu.make_async_remote_copy(
            src_ref=outbox[n].at[part, pl.ds(base, blocks)],
            dst_ref=inbox[n].at[part, pl.ds(base, blocks)],
            send_sem=rsend.at[s, k],
            recv_sem=rrecv.at[s, k],
            device_id=(partner(order[k])[1], side),
            device_id_type=MESH,
        )

    def first_rows(part, order, i, bit):
        natural = sum(((i >> (steps - 1 - n)) & 1) << order[n] for n in range(1, steps))
        first = part * per_part + (natural + bit * (1 << order[0])) * own
        return pl.ds(pl.multiple_of(first, own), own)

    def send(s, k):
        part, n, lane0, width, order = streams[s]
        theirs = 1 - partner(order[k])[0]
        blocks = chips >> (k + 1)
        base = chips - (chips >> k)
        before = chips - (chips >> (k - 1)) if k else 0
        for i in range(blocks):
            if k == 0:
                sent = acc[first_rows(part, order, i, theirs), pl.ds(lane0, width)]
            else:
                sent = work[n][part, before + theirs * blocks + i]
            outbox[n][part, base + i] = sent.astype(jnp.bfloat16)
        exchange(s, k).start()

    def receive(s, k):
        part, n, lane0, width, order = streams[s]
        mine = partner(order[k])[0]
        blocks = chips >> (k + 1)
        base = chips - (chips >> k)
        before = chips - (chips >> (k - 1)) if k else 0
        exchange(s, k).wait_recv()
        for i in range(blocks):
            if k == 0:
                kept = acc[first_rows(part, order, i, mine), pl.ds(lane0, width)]
            else:
                kept = work[n][part, before + mine * blocks + i]
            work[n][part, base + i] = kept + inbox[n][part, base + i].astype(jnp.float32)

    def own_day(day):
        for off in range(1, halves):
            gather(day, off).wait_recv()
            forward(day, off).start()
        correlate(core, day, 0, rows)
        direct(day).wait_recv()
        for off in range(1, halves):
            forward(day, off).wait_recv()

    def one_day(day, carry):
        own_day(day)
        correlate(1 - core, day, 0, rows)
        return carry

    lax.fori_loop(0, days - 1, one_day, 0)
    own_day(days - 1)
    for part in range(parts):
        here = pl.ds(part * per_part, per_part)
        correlate(1 - core, days - 1, part * per_part, per_part)
        acc[here, 6 * 128 :] = packed_rest([tail[j, here] for j in range(6)], count[here])
        for s in range(len(streams)):
            if streams[s][0] == part:
                send(s, 0)
    for k in range(steps):
        for s in range(len(streams)):
            receive(s, k)
            if k + 1 < steps:
                send(s, k + 1)

    last = chips - 2
    whole = jnp.concatenate(
        [
            jnp.concatenate([work[n][part, last] for n in range(len(SHARES))], 1)
            for part in range(parts)
        ],
        0,
    )
    sums, total = unpacked(whole)
    linear = [sums[back] / total for back in range(2)]
    weighted = [
        linear[back]
        * (sums[2 + back] * sums[2 + back] + sums[4 + back] * sums[4 + back])
        / (total * total)
        for back in range(2)
    ]
    ordered = in_order(
        *(jnp.concatenate([linear[back], weighted[back]], 0) for back in range(2)), turn[...]
    )
    lin_out[...] = ordered[: own * parts]
    wgt_out[...] = ordered[own * parts :]
    mask_copy.wait_send()
    for day in range(days):
        direct(day).wait_send()
        for off in range(1, halves):
            gather(day, off).wait_send()
            forward(day, off).wait_send()
    for s in range(len(streams)):
        for k in range(steps):
            exchange(s, k).wait_send()


def per_device(spectra, pair_list, mask, *, groups, halves):
    days, local, width = spectra.shape
    chips = groups // 2
    rows = pair_list.shape[0] // 2
    parts = parts_of(rows // chips)
    own = rows // chips // parts
    steps = chips.bit_length() - 1
    streams = len(streams_of(steps, parts))
    stations = local * halves
    operands = (spectra, pair_list.T, mask, jnp.asarray(lag_table()))
    hbm = pl.BlockSpec(memory_space=pltpu.HBM)
    vmem = pl.BlockSpec(memory_space=pltpu.VMEM)
    lin, wgt = pl.pallas_call(
        functools.partial(kernel, chips, halves),
        out_shape=[jax.ShapeDtypeStruct((own * parts, LANES), jnp.float32)] * 2,
        in_specs=[hbm] * 4,
        out_specs=[vmem, vmem],
        scratch_shapes=[
            pltpu.VMEM((2, days, stations, width), jnp.bfloat16),
            pltpu.VMEM((F, 2 * WIDE), jnp.bfloat16),
            pltpu.VMEM((2, 2 * rows), jnp.int32),
            pltpu.VMEM((2, *mask.shape), jnp.int32),
            pltpu.VMEM((2 * rows, stations), jnp.float32),
            pltpu.VMEM((2, rows, stations), jnp.float32),
            pltpu.VMEM((rows, PACKED), jnp.float32),
            pltpu.VMEM((6, rows, 128), jnp.float32),
            pltpu.VMEM((rows, 128), jnp.float32),
            pltpu.VMEM((WIDE, WIDE), jnp.bfloat16),
            *(
                pltpu.VMEM((parts, chips, own, share), dtype)
                for dtype in (jnp.float32, jnp.bfloat16, jnp.bfloat16)
                for share in SHARES
            ),
            pltpu.SemaphoreType.DMA((4,)),
            pltpu.SemaphoreType.DMA((days, halves - 1)),
            pltpu.SemaphoreType.DMA((days, halves - 1)),
            pltpu.SemaphoreType.DMA((days, halves - 1)),
            pltpu.SemaphoreType.DMA((days, halves - 1)),
            pltpu.SemaphoreType.DMA((days + 1,)),
            pltpu.SemaphoreType.DMA((days + 1,)),
            pltpu.SemaphoreType.DMA((streams, steps)),
            pltpu.SemaphoreType.DMA((streams, steps)),
        ],
        compiler_params=pltpu.CompilerParams(
            collective_id=0, has_side_effects=True, vmem_limit_bytes=VMEM_LIMIT
        ),
    )(*[pltpu.with_memory_space_constraint(x, pltpu.HBM) for x in operands])
    return lin[:, :LAGS].T, wgt[:, :LAGS].T


def solution(mesh):
    in_specs = (P("day", "pair", None), P("pair", None), P("day", None))
    out_specs = (P(None, ("pair", "day")), P(None, ("pair", "day")))
    return jax.shard_map(
        functools.partial(per_device, groups=mesh.shape["day"], halves=mesh.shape["pair"]),
        mesh=mesh,
        in_specs=in_specs,
        out_specs=out_specs,
        check_vma=False,
    )
```

```python
import functools
import math

import jax
import jax.numpy as jnp
import ml_dtypes
import numpy as np
from jax import lax
from jax.experimental import pallas as pl
from jax.experimental.pallas import tpu as pltpu
from jax.sharding import PartitionSpec as P

F = 512
MAXLAG = 200
LAGS = 401
LANES = 512
WIDE = 256
PACKED = 1280
SHARES = (384, 256, 384, 256)
AHEAD = 2
MESH = pl.DeviceIdType.MESH
VMEM_LIMIT = 40 * 1024 * 1024


def lag_table():
    lag = np.arange(MAXLAG + 1)
    freq = np.arange(F)
    phase = np.mod(lag[None, :] * freq[:, None], 2 * F) * (math.pi / F)
    table = np.zeros((F, 2 * WIDE), np.float32)
    table[:, : MAXLAG + 1] = np.cos(phase) / math.sqrt(F)
    table[:, WIDE : WIDE + MAXLAG + 1] = np.sin(phase) / math.sqrt(F)
    return table.astype(ml_dtypes.bfloat16)


def packed_rest(tail, count):
    lane = lax.broadcasted_iota(jnp.int32, count.shape, 1)
    tiles = [
        jnp.where(lane < 64, tail[2 * n], pltpu.roll(tail[2 * n + 1], 64, 1)) for n in range(3)
    ]
    ends = count
    for j in range(6):
        ends += pltpu.roll(jnp.where(lane >= 64, tail[j], 0.0), (16 * j + 64) % 128, 1)
    return jnp.concatenate(tiles + [ends], 1)


def unpacked(whole):
    tile = [whole[:, n * 128 : (n + 1) * 128] for n in range(PACKED // 128)]
    lane = lax.broadcasted_iota(jnp.int32, tile[0].shape, 1)
    sums = []
    for j in range(6):
        middle = tile[6 + j // 2] if j % 2 == 0 else pltpu.roll(tile[6 + j // 2], 64, 1)
        end = pltpu.roll(tile[9], (192 - 16 * j) % 128, 1)
        rest = jnp.where(lane < 64, middle, jnp.where(lane < 73, end, 0.0))
        sums.append(jnp.concatenate([tile[j], rest], 1))
    return sums, tile[9][:, 96:97]


def in_order(plus, minus, turn):
    rows = minus.shape[0]
    high = minus.astype(jnp.bfloat16)
    left = minus - high.astype(jnp.float32)
    middle = left.astype(jnp.bfloat16)
    low = (left - middle.astype(jnp.float32)).astype(jnp.bfloat16)
    terms = jnp.dot(
        jnp.concatenate([high, middle, low], 0), turn, preferred_element_type=jnp.float32
    )
    turned = terms[:rows] + terms[rows : 2 * rows] + terms[2 * rows :]
    near, far = (pltpu.roll(plus[:, n * 128 : (n + 1) * 128], 72, 1) for n in range(2))
    lane = lax.broadcasted_iota(jnp.int32, near.shape, 1)
    return jnp.concatenate(
        [
            turned[:, :128],
            jnp.where(lane < 72, turned[:, 128:], near),
            jnp.where(lane < 72, near, far),
            far,
        ],
        1,
    )


def parts_of(own):
    return 2 if own % 32 == 0 else 1


def parts_of(own):
    return 2 if own % 32 == 0 else 1


def streams_of(steps, parts):
    straight = list(range(steps))
    swapped = straight[1::-1] + straight[2:]
    return [
        (p, n, sum(SHARES[:n]), SHARES[n], swapped if n % 2 else straight)
        for p in range(parts)
        for n in range(len(SHARES))
    ]


def kernel(
    chips, halves, spectra, pairs_hbm, mask_hbm, table, lin_out, wgt_out,
    spec_all, table_v, pairs, mask, hot, pick, acc, tail, count, turn, *boxes_and_semaphores,
):
    kinds = len(SHARES)
    work, outbox, inbox = (boxes_and_semaphores[kinds * n : kinds * (n + 1)] for n in range(3))
    load_sem, gsend, grecv, fsend, frecv, dsend, drecv, rsend, rrecv = boxes_and_semaphores[3 * kinds :]
    days, local, _ = spectra.shape
    rows = acc.shape[0]
    steps = chips.bit_length() - 1
    parts = parts_of(rows // chips)
    per_part = rows // parts
    own = per_part // chips
    streams = streams_of(steps, parts)
    me = lax.axis_index("day")
    side = lax.axis_index("pair")
    core = lax.rem(me, 2)
    sibling = me + 1 - 2 * core

    def partner(bit):
        size = 2 << bit
        mine = lax.rem(lax.div(me, size), 2)
        return mine, me + (1 - 2 * mine) * size

    def stations_of(where):
        return pl.ds(pl.multiple_of(where * local, local), local)

    mine_rows = stations_of(side)
    loads = [
        pltpu.make_async_copy(pairs_hbm, pairs, load_sem.at[0]),
        pltpu.make_async_copy(mask_hbm, mask.at[core], load_sem.at[1]),
        pltpu.make_async_copy(spectra, spec_all.at[core, :, mine_rows, :], load_sem.at[2]),
        pltpu.make_async_copy(table, table_v, load_sem.at[3]),
    ]
    for copy in loads:
        copy.start()

    barrier = pltpu.get_barrier_semaphore()
    for off in range(1, halves):
        pl.semaphore_signal(
            barrier, inc=1, device_id=(me, lax.rem(side + off, halves)), device_id_type=MESH
        )
    pl.semaphore_signal(barrier, inc=1, device_id=(sibling, side), device_id_type=MESH)
    for bit in range(steps):
        pl.semaphore_signal(barrier, inc=1, device_id=(partner(bit)[1], side), device_id_type=MESH)
    pl.semaphore_wait(barrier, halves + steps)

    def gather(day, off):
        return pltpu.make_async_remote_copy(
            src_ref=spectra.at[day],
            dst_ref=spec_all.at[core, day, mine_rows, :],
            send_sem=gsend.at[day, off - 1],
            recv_sem=grecv.at[day, off - 1],
            device_id=(me, lax.rem(side + off, halves)),
            device_id_type=MESH,
        )

    def forward(day, off):
        here = spec_all.at[core, day, stations_of(lax.rem(side + halves - off, halves)), :]
        return pltpu.make_async_remote_copy(
            src_ref=here,
            dst_ref=here,
            send_sem=fsend.at[day, off - 1],
            recv_sem=frecv.at[day, off - 1],
            device_id=(sibling, side),
            device_id_type=MESH,
        )

    def direct(day):
        return pltpu.make_async_remote_copy(
            src_ref=spectra.at[day],
            dst_ref=spec_all.at[core, day, mine_rows, :],
            send_sem=dsend.at[day],
            recv_sem=drecv.at[day],
            device_id=(sibling, side),
            device_id_type=MESH,
        )

    mask_copy = pltpu.make_async_remote_copy(
        src_ref=mask_hbm,
        dst_ref=mask.at[core],
        send_sem=dsend.at[days],
        recv_sem=drecv.at[days],
        device_id=(sibling, side),
        device_id_type=MESH,
    )

    for day in range(days):
        if day < AHEAD:
            for off in range(1, halves):
                gather(day, off).start()
        if day == 0:
            mask_copy.start()
        direct(day).start()

    stations = local * halves
    loads[0].wait()
    for end in range(2):
        row = lax.broadcasted_iota(jnp.int32, (stations, 2 * rows), 0)
        hot[...] = (pairs[end : end + 1, :] == row).astype(jnp.float32).T
        for part in range(parts):
            for chip in range(chips):
                first = (2 * chip + core) * (own * parts) + part * own
                pick[end, pl.ds(part * per_part + chip * own, own)] = hot[
                    pl.ds(pl.multiple_of(first, own), own)
                ]
    acc[...] = jnp.zeros_like(acc)
    tail[...] = jnp.zeros_like(tail)
    loads[1].wait()
    mask_copy.wait_recv()
    alive = 0.0
    for owner in range(2):
        seen = [
            lax.dot_general(
                pick[end],
                mask[owner].astype(jnp.float32),
                (((1,), (1,)), ((), ())),
                preferred_element_type=jnp.float32,
            )
            for end in range(2)
        ]
        alive += jnp.sum(seen[0] * seen[1], 1, keepdims=True)
    lane = lax.broadcasted_iota(jnp.int32, (rows, 128), 1)
    count[...] = jnp.where(lane == 96, alive, 0.0)
    turn[...] = (
        (
            lax.broadcasted_iota(jnp.int32, (WIDE, WIDE), 0)
            + lax.broadcasted_iota(jnp.int32, (WIDE, WIDE), 1)
            == MAXLAG
        )
        .astype(jnp.float32)
        .astype(jnp.bfloat16)
    )
    loads[2].wait()
    loads[3].wait()

    def correlate(owner, day, start, size):
        today = mask[owner, pl.ds(day, 1), :].astype(jnp.float32)
        spec = spec_all[owner, day]
        here = pl.ds(start, size)
        both = jnp.dot(
            (pick[:, here] * today).astype(jnp.bfloat16).reshape(2 * size, spec.shape[0]),
            spec,
            preferred_element_type=jnp.float32,
        )
        left_re, left_im = both[:size, :F], both[:size, F:]
        right_re, right_im = both[size:, :F], both[size:, F:]
        cross = jnp.concatenate(
            [
                (left_re * right_re + left_im * right_im).astype(jnp.bfloat16),
                (left_im * right_re - left_re * right_im).astype(jnp.bfloat16),
            ],
            0,
        )
        waves = jnp.dot(cross, table_v[...], preferred_element_type=jnp.float32)
        re_cos, re_sin = waves[:size, :WIDE], waves[:size, WIDE:]
        im_cos, im_sin = waves[size:, :WIDE], waves[size:, WIDE:]
        for back in range(2):
            if back:
                trace, hilbert = re_cos + im_sin, im_cos - re_sin
            else:
                trace, hilbert = re_cos - im_sin, im_cos + re_sin
            inverse = lax.rsqrt(jnp.maximum(trace * trace + hilbert * hilbert, 0.25))
            for n, value in enumerate((trace, trace * inverse, hilbert * inverse)):
                j = 2 * n + back
                acc[here, j * 128 : (j + 1) * 128] += value[:, :128]
                tail[j, here] += value[:, 128:]

    def exchange(s, k):
        part, n, _, _, order = streams[s]
        blocks = chips >> (k + 1)
        base = chips - (chips >> k)
        return pltpu.make_async_remote_copy(
            src_ref=outbox[n].at[part, pl.ds(base, blocks)],
            dst_ref=inbox[n].at[part, pl.ds(base, blocks)],
            send_sem=rsend.at[s, k],
            recv_sem=rrecv.at[s, k],
            device_id=(partner(order[k])[1], side),
            device_id_type=MESH,
        )

    def first_rows(part, order, i, bit):
        natural = sum(((i >> (steps - 1 - n)) & 1) << order[n] for n in range(1, steps))
        first = part * per_part + (natural + bit * (1 << order[0])) * own
        return pl.ds(pl.multiple_of(first, own), own)

    def send(s, k):
        part, n, lane0, width, order = streams[s]
        theirs = 1 - partner(order[k])[0]
        blocks = chips >> (k + 1)
        base = chips - (chips >> k)
        before = chips - (chips >> (k - 1)) if k else 0
        for i in range(blocks):
            if k == 0:
                sent = acc[first_rows(part, order, i, theirs), pl.ds(lane0, width)]
            else:
                sent = work[n][part, before + theirs * blocks + i]
            outbox[n][part, base + i] = sent.astype(jnp.bfloat16)
        exchange(s, k).start()

    def receive(s, k):
        part, n, lane0, width, order = streams[s]
        mine = partner(order[k])[0]
        blocks = chips >> (k + 1)
        base = chips - (chips >> k)
        before = chips - (chips >> (k - 1)) if k else 0
        exchange(s, k).wait_recv()
        for i in range(blocks):
            if k == 0:
                kept = acc[first_rows(part, order, i, mine), pl.ds(lane0, width)]
            else:
                kept = work[n][part, before + mine * blocks + i]
            work[n][part, base + i] = kept + inbox[n][part, base + i].astype(jnp.float32)

    def own_day(day):
        for off in range(1, halves):
            gather(day, off).wait_recv()
            forward(day, off).start()

        @pl.when(day + AHEAD < days)
        def _():
            for off in range(1, halves):
                gather(day + AHEAD, off).start()

        correlate(core, day, 0, rows)
        direct(day).wait_recv()
        for off in range(1, halves):
            forward(day, off).wait_recv()

    def one_day(day, carry):
        own_day(day)
        correlate(1 - core, day, 0, rows)
        return carry

    lax.fori_loop(0, days - 1, one_day, 0)
    own_day(days - 1)
    for part in range(parts):
        here = pl.ds(part * per_part, per_part)
        correlate(1 - core, days - 1, part * per_part, per_part)
        acc[here, 6 * 128 :] = packed_rest([tail[j, here] for j in range(6)], count[here])
        for s in range(len(streams)):
            if streams[s][0] == part:
                send(s, 0)
    for k in range(steps):
        for s in range(len(streams)):
            receive(s, k)
            if k + 1 < steps:
                send(s, k + 1)

    last = chips - 2
    whole = jnp.concatenate(
        [
            jnp.concatenate([work[n][part, last] for n in range(len(SHARES))], 1)
            for part in range(parts)
        ],
        0,
    )
    sums, total = unpacked(whole)
    linear = [sums[back] / total for back in range(2)]
    weighted = [
        linear[back]
        * (sums[2 + back] * sums[2 + back] + sums[4 + back] * sums[4 + back])
        / (total * total)
        for back in range(2)
    ]
    ordered = in_order(
        *(jnp.concatenate([linear[back], weighted[back]], 0) for back in range(2)), turn[...]
    )
    lin_out[...] = ordered[: own * parts]
    wgt_out[...] = ordered[own * parts :]
    mask_copy.wait_send()
    for day in range(days):
        direct(day).wait_send()
        for off in range(1, halves):
            gather(day, off).wait_send()
            forward(day, off).wait_send()
    for s in range(len(streams)):
        for k in range(steps):
            exchange(s, k).wait_send()


def per_device(spectra, pair_list, mask, *, groups, halves):
    days, local, width = spectra.shape
    chips = groups // 2
    rows = pair_list.shape[0] // 2
    parts = parts_of(rows // chips)
    own = rows // chips // parts
    steps = chips.bit_length() - 1
    streams = len(streams_of(steps, parts))
    stations = local * halves
    operands = (spectra, pair_list.T, mask, jnp.asarray(lag_table()))
    hbm = pl.BlockSpec(memory_space=pltpu.HBM)
    vmem = pl.BlockSpec(memory_space=pltpu.VMEM)
    lin, wgt = pl.pallas_call(
        functools.partial(kernel, chips, halves),
        out_shape=[jax.ShapeDtypeStruct((own * parts, LANES), jnp.float32)] * 2,
        in_specs=[hbm] * 4,
        out_specs=[vmem, vmem],
        scratch_shapes=[
            pltpu.VMEM((2, days, stations, width), jnp.bfloat16),
            pltpu.VMEM((F, 2 * WIDE), jnp.bfloat16),
            pltpu.VMEM((2, 2 * rows), jnp.int32),
            pltpu.VMEM((2, *mask.shape), jnp.int32),
            pltpu.VMEM((2 * rows, stations), jnp.float32),
            pltpu.VMEM((2, rows, stations), jnp.float32),
            pltpu.VMEM((rows, PACKED), jnp.float32),
            pltpu.VMEM((6, rows, 128), jnp.float32),
            pltpu.VMEM((rows, 128), jnp.float32),
            pltpu.VMEM((WIDE, WIDE), jnp.bfloat16),
            *(
                pltpu.VMEM((parts, chips, own, share), dtype)
                for dtype in (jnp.float32, jnp.bfloat16, jnp.bfloat16)
                for share in SHARES
            ),
            pltpu.SemaphoreType.DMA((4,)),
            pltpu.SemaphoreType.DMA((days, halves - 1)),
            pltpu.SemaphoreType.DMA((days, halves - 1)),
            pltpu.SemaphoreType.DMA((days, halves - 1)),
            pltpu.SemaphoreType.DMA((days, halves - 1)),
            pltpu.SemaphoreType.DMA((days + 1,)),
            pltpu.SemaphoreType.DMA((days + 1,)),
            pltpu.SemaphoreType.DMA((streams, steps)),
            pltpu.SemaphoreType.DMA((streams, steps)),
        ],
        compiler_params=pltpu.CompilerParams(
            collective_id=0, has_side_effects=True, vmem_limit_bytes=VMEM_LIMIT
        ),
    )(*[pltpu.with_memory_space_constraint(x, pltpu.HBM) for x in operands])
    return lin[:, :LAGS].T, wgt[:, :LAGS].T


def solution(mesh):
    in_specs = (P("day", "pair", None), P("pair", None), P("day", None))
    out_specs = (P(None, ("pair", "day")), P(None, ("pair", "day")))
    return jax.shard_map(
        functools.partial(per_device, groups=mesh.shape["day"], halves=mesh.shape["pair"]),
        mesh=mesh,
        in_specs=in_specs,
        out_specs=out_specs,
        check_vma=False,
    )
```

```python
import functools
import math

import jax
import jax.numpy as jnp
import ml_dtypes
import numpy as np
from jax import lax
from jax.experimental import pallas as pl
from jax.experimental.pallas import tpu as pltpu
from jax.sharding import PartitionSpec as P

F = 512
MAXLAG = 200
LAGS = 401
LANES = 512
WIDE = 256
PACKED = 1280
SHARES = (384, 128, 512, 256)
AHEAD = 2
MESH = pl.DeviceIdType.MESH
VMEM_LIMIT = 40 * 1024 * 1024


def lag_table():
    lag = np.arange(MAXLAG + 1)
    freq = np.arange(F)
    phase = np.mod(lag[None, :] * freq[:, None], 2 * F) * (math.pi / F)
    table = np.zeros((F, 2 * WIDE), np.float32)
    table[:, : MAXLAG + 1] = np.cos(phase) / math.sqrt(F)
    table[:, WIDE : WIDE + MAXLAG + 1] = np.sin(phase) / math.sqrt(F)
    return table.astype(ml_dtypes.bfloat16)


def packed_rest(tail, count):
    lane = lax.broadcasted_iota(jnp.int32, count.shape, 1)
    tiles = [
        jnp.where(lane < 64, tail[2 * n], pltpu.roll(tail[2 * n + 1], 64, 1)) for n in range(3)
    ]
    ends = count
    for j in range(6):
        ends += pltpu.roll(jnp.where(lane >= 64, tail[j], 0.0), (16 * j + 64) % 128, 1)
    return jnp.concatenate(tiles + [ends], 1)


def unpacked(whole):
    tile = [whole[:, n * 128 : (n + 1) * 128] for n in range(PACKED // 128)]
    lane = lax.broadcasted_iota(jnp.int32, tile[0].shape, 1)
    sums = []
    for j in range(6):
        middle = tile[6 + j // 2] if j % 2 == 0 else pltpu.roll(tile[6 + j // 2], 64, 1)
        end = pltpu.roll(tile[9], (192 - 16 * j) % 128, 1)
        rest = jnp.where(lane < 64, middle, jnp.where(lane < 73, end, 0.0))
        sums.append(jnp.concatenate([tile[j], rest], 1))
    return sums, tile[9][:, 96:97]


def in_order(plus, minus, turn):
    rows = minus.shape[0]
    high = minus.astype(jnp.bfloat16)
    left = minus - high.astype(jnp.float32)
    middle = left.astype(jnp.bfloat16)
    low = (left - middle.astype(jnp.float32)).astype(jnp.bfloat16)
    terms = jnp.dot(
        jnp.concatenate([high, middle, low], 0), turn, preferred_element_type=jnp.float32
    )
    turned = terms[:rows] + terms[rows : 2 * rows] + terms[2 * rows :]
    near, far = (pltpu.roll(plus[:, n * 128 : (n + 1) * 128], 72, 1) for n in range(2))
    lane = lax.broadcasted_iota(jnp.int32, near.shape, 1)
    return jnp.concatenate(
        [
            turned[:, :128],
            jnp.where(lane < 72, turned[:, 128:], near),
            jnp.where(lane < 72, near, far),
            far,
        ],
        1,
    )


def parts_of(own):
    return 2 if own % 32 == 0 else 1


def parts_of(own):
    return 2 if own % 32 == 0 else 1


def streams_of(steps, parts):
    straight = list(range(steps))
    swapped = straight[1::-1] + straight[2:]
    return [
        (p, n, sum(SHARES[:n]), SHARES[n], swapped if n % 2 else straight)
        for p in range(parts)
        for n in range(len(SHARES))
    ]


def kernel(
    chips, halves, spectra, pairs_hbm, mask_hbm, table, lin_out, wgt_out,
    spec_all, table_v, pairs, mask, hot, pick, acc, tail, count, turn, *boxes_and_semaphores,
):
    kinds = len(SHARES)
    work, outbox, inbox = (boxes_and_semaphores[kinds * n : kinds * (n + 1)] for n in range(3))
    load_sem, gsend, grecv, fsend, frecv, dsend, drecv, rsend, rrecv = boxes_and_semaphores[3 * kinds :]
    days, local, _ = spectra.shape
    rows = acc.shape[0]
    steps = chips.bit_length() - 1
    parts = parts_of(rows // chips)
    per_part = rows // parts
    own = per_part // chips
    streams = streams_of(steps, parts)
    me = lax.axis_index("day")
    side = lax.axis_index("pair")
    core = lax.rem(me, 2)
    sibling = me + 1 - 2 * core

    def partner(bit):
        size = 2 << bit
        mine = lax.rem(lax.div(me, size), 2)
        return mine, me + (1 - 2 * mine) * size

    def stations_of(where):
        return pl.ds(pl.multiple_of(where * local, local), local)

    mine_rows = stations_of(side)
    loads = [
        pltpu.make_async_copy(pairs_hbm, pairs, load_sem.at[0]),
        pltpu.make_async_copy(mask_hbm, mask.at[core], load_sem.at[1]),
        pltpu.make_async_copy(spectra, spec_all.at[core, :, mine_rows, :], load_sem.at[2]),
        pltpu.make_async_copy(table, table_v, load_sem.at[3]),
    ]
    for copy in loads:
        copy.start()

    barrier = pltpu.get_barrier_semaphore()
    for off in range(1, halves):
        pl.semaphore_signal(
            barrier, inc=1, device_id=(me, lax.rem(side + off, halves)), device_id_type=MESH
        )
    pl.semaphore_signal(barrier, inc=1, device_id=(sibling, side), device_id_type=MESH)
    for bit in range(steps):
        pl.semaphore_signal(barrier, inc=1, device_id=(partner(bit)[1], side), device_id_type=MESH)
    pl.semaphore_wait(barrier, halves + steps)

    def gather(day, off):
        return pltpu.make_async_remote_copy(
            src_ref=spectra.at[day],
            dst_ref=spec_all.at[core, day, mine_rows, :],
            send_sem=gsend.at[day, off - 1],
            recv_sem=grecv.at[day, off - 1],
            device_id=(me, lax.rem(side + off, halves)),
            device_id_type=MESH,
        )

    def forward(day, off):
        here = spec_all.at[core, day, stations_of(lax.rem(side + halves - off, halves)), :]
        return pltpu.make_async_remote_copy(
            src_ref=here,
            dst_ref=here,
            send_sem=fsend.at[day, off - 1],
            recv_sem=frecv.at[day, off - 1],
            device_id=(sibling, side),
            device_id_type=MESH,
        )

    def direct(day):
        return pltpu.make_async_remote_copy(
            src_ref=spectra.at[day],
            dst_ref=spec_all.at[core, day, mine_rows, :],
            send_sem=dsend.at[day],
            recv_sem=drecv.at[day],
            device_id=(sibling, side),
            device_id_type=MESH,
        )

    mask_copy = pltpu.make_async_remote_copy(
        src_ref=mask_hbm,
        dst_ref=mask.at[core],
        send_sem=dsend.at[days],
        recv_sem=drecv.at[days],
        device_id=(sibling, side),
        device_id_type=MESH,
    )

    for day in range(days):
        if day < AHEAD:
            for off in range(1, halves):
                gather(day, off).start()
        if day == 0:
            mask_copy.start()
        direct(day).start()

    stations = local * halves
    loads[0].wait()
    for end in range(2):
        row = lax.broadcasted_iota(jnp.int32, (stations, 2 * rows), 0)
        hot[...] = (pairs[end : end + 1, :] == row).astype(jnp.float32).T
        for part in range(parts):
            for chip in range(chips):
                first = (2 * chip + core) * (own * parts) + part * own
                pick[end, pl.ds(part * per_part + chip * own, own)] = hot[
                    pl.ds(pl.multiple_of(first, own), own)
                ]
    acc[...] = jnp.zeros_like(acc)
    tail[...] = jnp.zeros_like(tail)
    loads[1].wait()
    mask_copy.wait_recv()
    alive = 0.0
    for owner in range(2):
        seen = [
            lax.dot_general(
                pick[end],
                mask[owner].astype(jnp.float32),
                (((1,), (1,)), ((), ())),
                preferred_element_type=jnp.float32,
            )
            for end in range(2)
        ]
        alive += jnp.sum(seen[0] * seen[1], 1, keepdims=True)
    lane = lax.broadcasted_iota(jnp.int32, (rows, 128), 1)
    count[...] = jnp.where(lane == 96, alive, 0.0)
    turn[...] = (
        (
            lax.broadcasted_iota(jnp.int32, (WIDE, WIDE), 0)
            + lax.broadcasted_iota(jnp.int32, (WIDE, WIDE), 1)
            == MAXLAG
        )
        .astype(jnp.float32)
        .astype(jnp.bfloat16)
    )
    loads[2].wait()
    loads[3].wait()

    def correlate(owner, day, start, size):
        today = mask[owner, pl.ds(day, 1), :].astype(jnp.float32)
        spec = spec_all[owner, day]
        here = pl.ds(start, size)
        both = jnp.dot(
            (pick[:, here] * today).astype(jnp.bfloat16).reshape(2 * size, spec.shape[0]),
            spec,
            preferred_element_type=jnp.float32,
        )
        left_re, left_im = both[:size, :F], both[:size, F:]
        right_re, right_im = both[size:, :F], both[size:, F:]
        cross = jnp.concatenate(
            [
                (left_re * right_re + left_im * right_im).astype(jnp.bfloat16),
                (left_im * right_re - left_re * right_im).astype(jnp.bfloat16),
            ],
            0,
        )
        waves = jnp.dot(cross, table_v[...], preferred_element_type=jnp.float32)
        re_cos, re_sin = waves[:size, :WIDE], waves[:size, WIDE:]
        im_cos, im_sin = waves[size:, :WIDE], waves[size:, WIDE:]
        for back in range(2):
            if back:
                trace, hilbert = re_cos + im_sin, im_cos - re_sin
            else:
                trace, hilbert = re_cos - im_sin, im_cos + re_sin
            inverse = lax.rsqrt(jnp.maximum(trace * trace + hilbert * hilbert, 0.25))
            for n, value in enumerate((trace, trace * inverse, hilbert * inverse)):
                j = 2 * n + back
                acc[here, j * 128 : (j + 1) * 128] += value[:, :128]
                tail[j, here] += value[:, 128:]

    def exchange(s, k):
        part, n, _, _, order = streams[s]
        blocks = chips >> (k + 1)
        base = chips - (chips >> k)
        return pltpu.make_async_remote_copy(
            src_ref=outbox[n].at[part, pl.ds(base, blocks)],
            dst_ref=inbox[n].at[part, pl.ds(base, blocks)],
            send_sem=rsend.at[s, k],
            recv_sem=rrecv.at[s, k],
            device_id=(partner(order[k])[1], side),
            device_id_type=MESH,
        )

    def first_rows(part, order, i, bit):
        natural = sum(((i >> (steps - 1 - n)) & 1) << order[n] for n in range(1, steps))
        first = part * per_part + (natural + bit * (1 << order[0])) * own
        return pl.ds(pl.multiple_of(first, own), own)

    def send(s, k):
        part, n, lane0, width, order = streams[s]
        theirs = 1 - partner(order[k])[0]
        blocks = chips >> (k + 1)
        base = chips - (chips >> k)
        before = chips - (chips >> (k - 1)) if k else 0
        for i in range(blocks):
            if k == 0:
                sent = acc[first_rows(part, order, i, theirs), pl.ds(lane0, width)]
            else:
                sent = work[n][part, before + theirs * blocks + i]
            outbox[n][part, base + i] = sent.astype(jnp.bfloat16)
        exchange(s, k).start()

    def receive(s, k):
        part, n, lane0, width, order = streams[s]
        mine = partner(order[k])[0]
        blocks = chips >> (k + 1)
        base = chips - (chips >> k)
        before = chips - (chips >> (k - 1)) if k else 0
        exchange(s, k).wait_recv()
        for i in range(blocks):
            if k == 0:
                kept = acc[first_rows(part, order, i, mine), pl.ds(lane0, width)]
            else:
                kept = work[n][part, before + mine * blocks + i]
            work[n][part, base + i] = kept + inbox[n][part, base + i].astype(jnp.float32)

    def own_day(day):
        for off in range(1, halves):
            gather(day, off).wait_recv()
            forward(day, off).start()

        @pl.when(day + AHEAD < days)
        def _():
            for off in range(1, halves):
                gather(day + AHEAD, off).start()

        correlate(core, day, 0, rows)
        direct(day).wait_recv()
        for off in range(1, halves):
            forward(day, off).wait_recv()

    def one_day(day, carry):
        own_day(day)
        correlate(1 - core, day, 0, rows)
        return carry

    lax.fori_loop(0, days - 1, one_day, 0)
    own_day(days - 1)
    for part in range(parts):
        here = pl.ds(part * per_part, per_part)
        correlate(1 - core, days - 1, part * per_part, per_part)
        packed = False
        for s in range(len(streams)):
            if streams[s][0] == part:
                if not packed and streams[s][2] + streams[s][3] > 6 * 128:
                    acc[here, 6 * 128 :] = packed_rest([tail[j, here] for j in range(6)], count[here])
                    packed = True
                send(s, 0)

    def finish(part):
        whole = jnp.concatenate([work[n][part, chips - 2] for n in range(len(SHARES))], 1)
        sums, total = unpacked(whole)
        linear = [sums[back] / total for back in range(2)]
        weighted = [
            linear[back]
            * (sums[2 + back] * sums[2 + back] + sums[4 + back] * sums[4 + back])
            / (total * total)
            for back in range(2)
        ]
        ordered = in_order(
            *(jnp.concatenate([linear[back], weighted[back]], 0) for back in range(2)), turn[...]
        )
        here = pl.ds(part * own, own)
        lin_out[here] = ordered[:own]
        wgt_out[here] = ordered[own:]

    for k in range(steps):
        for s in range(len(streams)):
            receive(s, k)
            if k + 1 < steps:
                send(s, k + 1)
            elif s + 1 == len(streams) or streams[s + 1][0] != streams[s][0]:
                finish(streams[s][0])

    mask_copy.wait_send()
    for day in range(days):
        direct(day).wait_send()
        for off in range(1, halves):
            gather(day, off).wait_send()
            forward(day, off).wait_send()
    for s in range(len(streams)):
        for k in range(steps):
            exchange(s, k).wait_send()


def per_device(spectra, pair_list, mask, *, groups, halves):
    days, local, width = spectra.shape
    chips = groups // 2
    rows = pair_list.shape[0] // 2
    parts = parts_of(rows // chips)
    own = rows // chips // parts
    steps = chips.bit_length() - 1
    streams = len(streams_of(steps, parts))
    stations = local * halves
    operands = (spectra, pair_list.T, mask, jnp.asarray(lag_table()))
    hbm = pl.BlockSpec(memory_space=pltpu.HBM)
    vmem = pl.BlockSpec(memory_space=pltpu.VMEM)
    lin, wgt = pl.pallas_call(
        functools.partial(kernel, chips, halves),
        out_shape=[jax.ShapeDtypeStruct((own * parts, LANES), jnp.float32)] * 2,
        in_specs=[hbm] * 4,
        out_specs=[vmem, vmem],
        scratch_shapes=[
            pltpu.VMEM((2, days, stations, width), jnp.bfloat16),
            pltpu.VMEM((F, 2 * WIDE), jnp.bfloat16),
            pltpu.VMEM((2, 2 * rows), jnp.int32),
            pltpu.VMEM((2, *mask.shape), jnp.int32),
            pltpu.VMEM((2 * rows, stations), jnp.float32),
            pltpu.VMEM((2, rows, stations), jnp.float32),
            pltpu.VMEM((rows, PACKED), jnp.float32),
            pltpu.VMEM((6, rows, 128), jnp.float32),
            pltpu.VMEM((rows, 128), jnp.float32),
            pltpu.VMEM((WIDE, WIDE), jnp.bfloat16),
            *(
                pltpu.VMEM((parts, chips, own, share), dtype)
                for dtype in (jnp.float32, jnp.bfloat16, jnp.bfloat16)
                for share in SHARES
            ),
            pltpu.SemaphoreType.DMA((4,)),
            pltpu.SemaphoreType.DMA((days, halves - 1)),
            pltpu.SemaphoreType.DMA((days, halves - 1)),
            pltpu.SemaphoreType.DMA((days, halves - 1)),
            pltpu.SemaphoreType.DMA((days, halves - 1)),
            pltpu.SemaphoreType.DMA((days + 1,)),
            pltpu.SemaphoreType.DMA((days + 1,)),
            pltpu.SemaphoreType.DMA((streams, steps)),
            pltpu.SemaphoreType.DMA((streams, steps)),
        ],
        compiler_params=pltpu.CompilerParams(
            collective_id=0, has_side_effects=True, vmem_limit_bytes=VMEM_LIMIT
        ),
    )(*[pltpu.with_memory_space_constraint(x, pltpu.HBM) for x in operands])
    return lin[:, :LAGS].T, wgt[:, :LAGS].T


def solution(mesh):
    in_specs = (P("day", "pair", None), P("pair", None), P("day", None))
    out_specs = (P(None, ("pair", "day")), P(None, ("pair", "day")))
    return jax.shard_map(
        functools.partial(per_device, groups=mesh.shape["day"], halves=mesh.shape["pair"]),
        mesh=mesh,
        in_specs=in_specs,
        out_specs=out_specs,
        check_vma=False,
    )
```

```python
import functools
import math

import jax
import jax.numpy as jnp
import ml_dtypes
import numpy as np
from jax import lax
from jax.experimental import pallas as pl
from jax.experimental.pallas import tpu as pltpu
from jax.sharding import PartitionSpec as P

F = 512
MAXLAG = 200
LAGS = 401
LANES = 512
WIDE = 256
PACKED = 1280
SHARES = (256, 384, 256, 384)
AHEAD = 2
MESH = pl.DeviceIdType.MESH
VMEM_LIMIT = 40 * 1024 * 1024


def lag_table():
    lag = np.arange(MAXLAG + 1)
    freq = np.arange(F)
    phase = np.mod(lag[None, :] * freq[:, None], 2 * F) * (math.pi / F)
    table = np.zeros((F, 2 * WIDE), np.float32)
    table[:, : MAXLAG + 1] = np.cos(phase) / math.sqrt(F)
    table[:, WIDE : WIDE + MAXLAG + 1] = np.sin(phase) / math.sqrt(F)
    return table.astype(ml_dtypes.bfloat16)


def packed_rest(tail, count):
    lane = lax.broadcasted_iota(jnp.int32, count.shape, 1)
    tiles = [
        jnp.where(lane < 64, tail[2 * n], pltpu.roll(tail[2 * n + 1], 64, 1)) for n in range(3)
    ]
    ends = count
    for j in range(6):
        ends += pltpu.roll(jnp.where(lane >= 64, tail[j], 0.0), (16 * j + 64) % 128, 1)
    return jnp.concatenate(tiles + [ends], 1)


def unpacked(whole):
    tile = [whole[:, n * 128 : (n + 1) * 128] for n in range(PACKED // 128)]
    lane = lax.broadcasted_iota(jnp.int32, tile[0].shape, 1)
    sums = []
    for j in range(6):
        middle = tile[6 + j // 2] if j % 2 == 0 else pltpu.roll(tile[6 + j // 2], 64, 1)
        end = pltpu.roll(tile[9], (192 - 16 * j) % 128, 1)
        rest = jnp.where(lane < 64, middle, jnp.where(lane < 73, end, 0.0))
        sums.append(jnp.concatenate([tile[j], rest], 1))
    return sums, tile[9][:, 96:97]


def in_order(plus, minus, turn):
    rows = minus.shape[0]
    high = minus.astype(jnp.bfloat16)
    left = minus - high.astype(jnp.float32)
    middle = left.astype(jnp.bfloat16)
    low = (left - middle.astype(jnp.float32)).astype(jnp.bfloat16)
    terms = jnp.dot(
        jnp.concatenate([high, middle, low], 0), turn, preferred_element_type=jnp.float32
    )
    turned = terms[:rows] + terms[rows : 2 * rows] + terms[2 * rows :]
    near, far = (pltpu.roll(plus[:, n * 128 : (n + 1) * 128], 72, 1) for n in range(2))
    lane = lax.broadcasted_iota(jnp.int32, near.shape, 1)
    return jnp.concatenate(
        [
            turned[:, :128],
            jnp.where(lane < 72, turned[:, 128:], near),
            jnp.where(lane < 72, near, far),
            far,
        ],
        1,
    )


def parts_of(own):
    return 2 if own % 32 == 0 else 1


def parts_of(own):
    return 2 if own % 32 == 0 else 1


def streams_of(steps, parts):
    straight = list(range(steps))
    swapped = straight[1::-1] + straight[2:]
    return [
        (p, n, sum(SHARES[:n]), SHARES[n], swapped if n % 2 else straight)
        for p in range(parts)
        for n in range(len(SHARES))
    ]


def kernel(
    chips, halves, spectra, pairs_hbm, mask_hbm, table, lin_out, wgt_out,
    spec_all, table_v, pairs, mask, hot, pick, acc, tail, count, turn, *boxes_and_semaphores,
):
    kinds = len(SHARES)
    work, outbox, inbox = (boxes_and_semaphores[kinds * n : kinds * (n + 1)] for n in range(3))
    load_sem, gsend, grecv, fsend, frecv, dsend, drecv, rsend, rrecv = boxes_and_semaphores[3 * kinds :]
    days, local, _ = spectra.shape
    rows = acc.shape[0]
    steps = chips.bit_length() - 1
    parts = parts_of(rows // chips)
    per_part = rows // parts
    own = per_part // chips
    streams = streams_of(steps, parts)
    me = lax.axis_index("day")
    side = lax.axis_index("pair")
    core = lax.rem(me, 2)
    sibling = me + 1 - 2 * core

    def partner(bit):
        size = 2 << bit
        mine = lax.rem(lax.div(me, size), 2)
        return mine, me + (1 - 2 * mine) * size

    def stations_of(where):
        return pl.ds(pl.multiple_of(where * local, local), local)

    mine_rows = stations_of(side)
    loads = [
        pltpu.make_async_copy(pairs_hbm, pairs, load_sem.at[0]),
        pltpu.make_async_copy(mask_hbm, mask.at[core], load_sem.at[1]),
        pltpu.make_async_copy(spectra, spec_all.at[core, :, mine_rows, :], load_sem.at[2]),
        pltpu.make_async_copy(table, table_v, load_sem.at[3]),
    ]
    for copy in loads:
        copy.start()

    barrier = pltpu.get_barrier_semaphore()
    for off in range(1, halves):
        pl.semaphore_signal(
            barrier, inc=1, device_id=(me, lax.rem(side + off, halves)), device_id_type=MESH
        )
    pl.semaphore_signal(barrier, inc=1, device_id=(sibling, side), device_id_type=MESH)
    for bit in range(steps):
        pl.semaphore_signal(barrier, inc=1, device_id=(partner(bit)[1], side), device_id_type=MESH)
    pl.semaphore_wait(barrier, halves + steps)

    def gather(day, off):
        return pltpu.make_async_remote_copy(
            src_ref=spectra.at[day],
            dst_ref=spec_all.at[core, day, mine_rows, :],
            send_sem=gsend.at[day, off - 1],
            recv_sem=grecv.at[day, off - 1],
            device_id=(me, lax.rem(side + off, halves)),
            device_id_type=MESH,
        )

    def forward(day, off):
        here = spec_all.at[core, day, stations_of(lax.rem(side + halves - off, halves)), :]
        return pltpu.make_async_remote_copy(
            src_ref=here,
            dst_ref=here,
            send_sem=fsend.at[day, off - 1],
            recv_sem=frecv.at[day, off - 1],
            device_id=(sibling, side),
            device_id_type=MESH,
        )

    def direct(day):
        return pltpu.make_async_remote_copy(
            src_ref=spectra.at[day],
            dst_ref=spec_all.at[core, day, mine_rows, :],
            send_sem=dsend.at[day],
            recv_sem=drecv.at[day],
            device_id=(sibling, side),
            device_id_type=MESH,
        )

    mask_copy = pltpu.make_async_remote_copy(
        src_ref=mask_hbm,
        dst_ref=mask.at[core],
        send_sem=dsend.at[days],
        recv_sem=drecv.at[days],
        device_id=(sibling, side),
        device_id_type=MESH,
    )

    for day in range(days):
        if day < AHEAD:
            for off in range(1, halves):
                gather(day, off).start()
        if day == 0:
            mask_copy.start()
        direct(day).start()

    stations = local * halves
    loads[0].wait()
    for end in range(2):
        row = lax.broadcasted_iota(jnp.int32, (stations, 2 * rows), 0)
        hot[...] = (pairs[end : end + 1, :] == row).astype(jnp.float32).T
        for part in range(parts):
            for chip in range(chips):
                first = (2 * chip + core) * (own * parts) + part * own
                pick[end, pl.ds(part * per_part + chip * own, own)] = hot[
                    pl.ds(pl.multiple_of(first, own), own)
                ]
    acc[...] = jnp.zeros_like(acc)
    tail[...] = jnp.zeros_like(tail)
    loads[1].wait()
    mask_copy.wait_recv()
    alive = 0.0
    for owner in range(2):
        seen = [
            lax.dot_general(
                pick[end],
                mask[owner].astype(jnp.float32),
                (((1,), (1,)), ((), ())),
                preferred_element_type=jnp.float32,
            )
            for end in range(2)
        ]
        alive += jnp.sum(seen[0] * seen[1], 1, keepdims=True)
    lane = lax.broadcasted_iota(jnp.int32, (rows, 128), 1)
    count[...] = jnp.where(lane == 96, alive, 0.0)
    turn[...] = (
        (
            lax.broadcasted_iota(jnp.int32, (WIDE, WIDE), 0)
            + lax.broadcasted_iota(jnp.int32, (WIDE, WIDE), 1)
            == MAXLAG
        )
        .astype(jnp.float32)
        .astype(jnp.bfloat16)
    )
    loads[2].wait()
    loads[3].wait()

    def correlate(owner, day, start, size):
        today = mask[owner, pl.ds(day, 1), :].astype(jnp.float32)
        spec = spec_all[owner, day]
        here = pl.ds(start, size)
        both = jnp.dot(
            (pick[:, here] * today).astype(jnp.bfloat16).reshape(2 * size, spec.shape[0]),
            spec,
            preferred_element_type=jnp.float32,
        )
        left_re, left_im = both[:size, :F], both[:size, F:]
        right_re, right_im = both[size:, :F], both[size:, F:]
        cross = jnp.concatenate(
            [
                (left_re * right_re + left_im * right_im).astype(jnp.bfloat16),
                (left_im * right_re - left_re * right_im).astype(jnp.bfloat16),
            ],
            0,
        )
        waves = jnp.dot(cross, table_v[...], preferred_element_type=jnp.float32)
        re_cos, re_sin = waves[:size, :WIDE], waves[:size, WIDE:]
        im_cos, im_sin = waves[size:, :WIDE], waves[size:, WIDE:]
        for back in range(2):
            if back:
                trace, hilbert = re_cos + im_sin, im_cos - re_sin
            else:
                trace, hilbert = re_cos - im_sin, im_cos + re_sin
            inverse = lax.rsqrt(jnp.maximum(trace * trace + hilbert * hilbert, 0.25))
            for n, value in enumerate((trace, trace * inverse, hilbert * inverse)):
                j = 2 * n + back
                acc[here, j * 128 : (j + 1) * 128] += value[:, :128]
                tail[j, here] += value[:, 128:]

    def exchange(s, k):
        part, n, _, _, order = streams[s]
        blocks = chips >> (k + 1)
        base = chips - (chips >> k)
        return pltpu.make_async_remote_copy(
            src_ref=outbox[n].at[part, pl.ds(base, blocks)],
            dst_ref=inbox[n].at[part, pl.ds(base, blocks)],
            send_sem=rsend.at[s, k],
            recv_sem=rrecv.at[s, k],
            device_id=(partner(order[k])[1], side),
            device_id_type=MESH,
        )

    def first_rows(part, order, i, bit):
        natural = sum(((i >> (steps - 1 - n)) & 1) << order[n] for n in range(1, steps))
        first = part * per_part + (natural + bit * (1 << order[0])) * own
        return pl.ds(pl.multiple_of(first, own), own)

    def send(s, k):
        part, n, lane0, width, order = streams[s]
        theirs = 1 - partner(order[k])[0]
        blocks = chips >> (k + 1)
        base = chips - (chips >> k)
        before = chips - (chips >> (k - 1)) if k else 0
        for i in range(blocks):
            if k == 0:
                sent = acc[first_rows(part, order, i, theirs), pl.ds(lane0, width)]
            else:
                sent = work[n][part, before + theirs * blocks + i]
            outbox[n][part, base + i] = sent.astype(jnp.bfloat16)
        exchange(s, k).start()

    def receive(s, k):
        part, n, lane0, width, order = streams[s]
        mine = partner(order[k])[0]
        blocks = chips >> (k + 1)
        base = chips - (chips >> k)
        before = chips - (chips >> (k - 1)) if k else 0
        exchange(s, k).wait_recv()
        for i in range(blocks):
            if k == 0:
                kept = acc[first_rows(part, order, i, mine), pl.ds(lane0, width)]
            else:
                kept = work[n][part, before + mine * blocks + i]
            work[n][part, base + i] = kept + inbox[n][part, base + i].astype(jnp.float32)

    def own_day(day):
        for off in range(1, halves):
            gather(day, off).wait_recv()
            forward(day, off).start()

        @pl.when(day + AHEAD < days)
        def _():
            for off in range(1, halves):
                gather(day + AHEAD, off).start()

        correlate(core, day, 0, rows)
        direct(day).wait_recv()
        for off in range(1, halves):
            forward(day, off).wait_recv()

    def one_day(day, carry):
        own_day(day)
        correlate(1 - core, day, 0, rows)
        return carry

    lax.fori_loop(0, days - 1, one_day, 0)
    own_day(days - 1)
    for part in range(parts):
        here = pl.ds(part * per_part, per_part)
        correlate(1 - core, days - 1, part * per_part, per_part)
        packed = False
        for s in range(len(streams)):
            if streams[s][0] == part:
                if not packed and streams[s][2] + streams[s][3] > 6 * 128:
                    acc[here, 6 * 128 :] = packed_rest([tail[j, here] for j in range(6)], count[here])
                    packed = True
                send(s, 0)

    def finish(part):
        whole = jnp.concatenate([work[n][part, chips - 2] for n in range(len(SHARES))], 1)
        sums, total = unpacked(whole)
        linear = [sums[back] / total for back in range(2)]
        weighted = [
            linear[back]
            * (sums[2 + back] * sums[2 + back] + sums[4 + back] * sums[4 + back])
            / (total * total)
            for back in range(2)
        ]
        ordered = in_order(
            *(jnp.concatenate([linear[back], weighted[back]], 0) for back in range(2)), turn[...]
        )
        here = pl.ds(part * own, own)
        lin_out[here] = ordered[:own]
        wgt_out[here] = ordered[own:]

    for k in range(steps):
        for s in range(len(streams)):
            receive(s, k)
            if k + 1 < steps:
                send(s, k + 1)
            elif s + 1 == len(streams) or streams[s + 1][0] != streams[s][0]:
                finish(streams[s][0])

    mask_copy.wait_send()
    for day in range(days):
        direct(day).wait_send()
        for off in range(1, halves):
            gather(day, off).wait_send()
            forward(day, off).wait_send()
    for s in range(len(streams)):
        for k in range(steps):
            exchange(s, k).wait_send()


def per_device(spectra, pair_list, mask, *, groups, halves):
    days, local, width = spectra.shape
    chips = groups // 2
    rows = pair_list.shape[0] // 2
    parts = parts_of(rows // chips)
    own = rows // chips // parts
    steps = chips.bit_length() - 1
    streams = len(streams_of(steps, parts))
    stations = local * halves
    operands = (spectra, pair_list.T, mask, jnp.asarray(lag_table()))
    hbm = pl.BlockSpec(memory_space=pltpu.HBM)
    vmem = pl.BlockSpec(memory_space=pltpu.VMEM)
    lin, wgt = pl.pallas_call(
        functools.partial(kernel, chips, halves),
        out_shape=[jax.ShapeDtypeStruct((own * parts, LANES), jnp.float32)] * 2,
        in_specs=[hbm] * 4,
        out_specs=[vmem, vmem],
        scratch_shapes=[
            pltpu.VMEM((2, days, stations, width), jnp.bfloat16),
            pltpu.VMEM((F, 2 * WIDE), jnp.bfloat16),
            pltpu.VMEM((2, 2 * rows), jnp.int32),
            pltpu.VMEM((2, *mask.shape), jnp.int32),
            pltpu.VMEM((2 * rows, stations), jnp.float32),
            pltpu.VMEM((2, rows, stations), jnp.float32),
            pltpu.VMEM((rows, PACKED), jnp.float32),
            pltpu.VMEM((6, rows, 128), jnp.float32),
            pltpu.VMEM((rows, 128), jnp.float32),
            pltpu.VMEM((WIDE, WIDE), jnp.bfloat16),
            *(
                pltpu.VMEM((parts, chips, own, share), dtype)
                for dtype in (jnp.float32, jnp.bfloat16, jnp.bfloat16)
                for share in SHARES
            ),
            pltpu.SemaphoreType.DMA((4,)),
            pltpu.SemaphoreType.DMA((days, halves - 1)),
            pltpu.SemaphoreType.DMA((days, halves - 1)),
            pltpu.SemaphoreType.DMA((days, halves - 1)),
            pltpu.SemaphoreType.DMA((days, halves - 1)),
            pltpu.SemaphoreType.DMA((days + 1,)),
            pltpu.SemaphoreType.DMA((days + 1,)),
            pltpu.SemaphoreType.DMA((streams, steps)),
            pltpu.SemaphoreType.DMA((streams, steps)),
        ],
        compiler_params=pltpu.CompilerParams(
            collective_id=0, has_side_effects=True, vmem_limit_bytes=VMEM_LIMIT
        ),
    )(*[pltpu.with_memory_space_constraint(x, pltpu.HBM) for x in operands])
    return lin[:, :LAGS].T, wgt[:, :LAGS].T


def solution(mesh):
    in_specs = (P("day", "pair", None), P("pair", None), P("day", None))
    out_specs = (P(None, ("pair", "day")), P(None, ("pair", "day")))
    return jax.shard_map(
        functools.partial(per_device, groups=mesh.shape["day"], halves=mesh.shape["pair"]),
        mesh=mesh,
        in_specs=in_specs,
        out_specs=out_specs,
        check_vma=False,
    )
```

```python
import functools
import math

import jax
import jax.numpy as jnp
import ml_dtypes
import numpy as np
from jax import lax
from jax.experimental import pallas as pl
from jax.experimental.pallas import tpu as pltpu
from jax.sharding import PartitionSpec as P

F = 512
MAXLAG = 200
LAGS = 401
LANES = 512
WIDE = 256
PACKED = 1280
SHARES = (384, 384, 256, 256)
AHEAD = 3
MESH = pl.DeviceIdType.MESH
VMEM_LIMIT = 40 * 1024 * 1024


def lag_table():
    lag = np.arange(MAXLAG + 1)
    freq = np.arange(F)
    phase = np.mod(lag[None, :] * freq[:, None], 2 * F) * (math.pi / F)
    table = np.zeros((F, 2 * WIDE), np.float32)
    table[:, : MAXLAG + 1] = np.cos(phase) / math.sqrt(F)
    table[:, WIDE : WIDE + MAXLAG + 1] = np.sin(phase) / math.sqrt(F)
    return table.astype(ml_dtypes.bfloat16)


def packed_rest(tail, count):
    lane = lax.broadcasted_iota(jnp.int32, count.shape, 1)
    tiles = [
        jnp.where(lane < 64, tail[2 * n], pltpu.roll(tail[2 * n + 1], 64, 1)) for n in range(3)
    ]
    ends = count
    for j in range(6):
        ends += pltpu.roll(jnp.where(lane >= 64, tail[j], 0.0), (16 * j + 64) % 128, 1)
    return jnp.concatenate(tiles + [ends], 1)


def unpacked(whole):
    tile = [whole[:, n * 128 : (n + 1) * 128] for n in range(PACKED // 128)]
    lane = lax.broadcasted_iota(jnp.int32, tile[0].shape, 1)
    sums = []
    for j in range(6):
        middle = tile[6 + j // 2] if j % 2 == 0 else pltpu.roll(tile[6 + j // 2], 64, 1)
        end = pltpu.roll(tile[9], (192 - 16 * j) % 128, 1)
        rest = jnp.where(lane < 64, middle, jnp.where(lane < 73, end, 0.0))
        sums.append(jnp.concatenate([tile[j], rest], 1))
    return sums, tile[9][:, 96:97]


def in_order(plus, minus, turn):
    rows = minus.shape[0]
    high = minus.astype(jnp.bfloat16)
    left = minus - high.astype(jnp.float32)
    middle = left.astype(jnp.bfloat16)
    low = (left - middle.astype(jnp.float32)).astype(jnp.bfloat16)
    terms = jnp.dot(
        jnp.concatenate([high, middle, low], 0), turn, preferred_element_type=jnp.float32
    )
    turned = terms[:rows] + terms[rows : 2 * rows] + terms[2 * rows :]
    near, far = (pltpu.roll(plus[:, n * 128 : (n + 1) * 128], 72, 1) for n in range(2))
    lane = lax.broadcasted_iota(jnp.int32, near.shape, 1)
    return jnp.concatenate(
        [
            turned[:, :128],
            jnp.where(lane < 72, turned[:, 128:], near),
            jnp.where(lane < 72, near, far),
            far,
        ],
        1,
    )


def parts_of(own):
    return 2 if own % 32 == 0 else 1


def parts_of(own):
    return 2 if own % 32 == 0 else 1


def streams_of(steps, parts):
    straight = list(range(steps))
    swapped = straight[1::-1] + straight[2:]
    return [
        (p, n, sum(SHARES[:n]), SHARES[n], swapped if n % 2 else straight)
        for p in range(parts)
        for n in range(len(SHARES))
    ]


def kernel(
    chips, halves, spectra, pairs_hbm, mask_hbm, table, lin_out, wgt_out,
    spec_all, table_v, pairs, mask, hot, pick, acc, tail, count, turn, *boxes_and_semaphores,
):
    kinds = len(SHARES)
    work, outbox, inbox = (boxes_and_semaphores[kinds * n : kinds * (n + 1)] for n in range(3))
    load_sem, gsend, grecv, fsend, frecv, dsend, drecv, rsend, rrecv = boxes_and_semaphores[3 * kinds :]
    days, local, _ = spectra.shape
    rows = acc.shape[0]
    steps = chips.bit_length() - 1
    parts = parts_of(rows // chips)
    per_part = rows // parts
    own = per_part // chips
    streams = streams_of(steps, parts)
    me = lax.axis_index("day")
    side = lax.axis_index("pair")
    core = lax.rem(me, 2)
    sibling = me + 1 - 2 * core

    def partner(bit):
        size = 2 << bit
        mine = lax.rem(lax.div(me, size), 2)
        return mine, me + (1 - 2 * mine) * size

    def stations_of(where):
        return pl.ds(pl.multiple_of(where * local, local), local)

    mine_rows = stations_of(side)
    loads = [
        pltpu.make_async_copy(pairs_hbm, pairs, load_sem.at[0]),
        pltpu.make_async_copy(mask_hbm, mask.at[core], load_sem.at[1]),
        pltpu.make_async_copy(spectra, spec_all.at[core, :, mine_rows, :], load_sem.at[2]),
        pltpu.make_async_copy(table, table_v, load_sem.at[3]),
    ]
    for copy in loads:
        copy.start()

    barrier = pltpu.get_barrier_semaphore()
    for off in range(1, halves):
        pl.semaphore_signal(
            barrier, inc=1, device_id=(me, lax.rem(side + off, halves)), device_id_type=MESH
        )
    pl.semaphore_signal(barrier, inc=1, device_id=(sibling, side), device_id_type=MESH)
    for bit in range(steps):
        pl.semaphore_signal(barrier, inc=1, device_id=(partner(bit)[1], side), device_id_type=MESH)
    pl.semaphore_wait(barrier, halves + steps)

    def gather(day, off):
        return pltpu.make_async_remote_copy(
            src_ref=spectra.at[day],
            dst_ref=spec_all.at[core, day, mine_rows, :],
            send_sem=gsend.at[day, off - 1],
            recv_sem=grecv.at[day, off - 1],
            device_id=(me, lax.rem(side + off, halves)),
            device_id_type=MESH,
        )

    def forward(day, off):
        here = spec_all.at[core, day, stations_of(lax.rem(side + halves - off, halves)), :]
        return pltpu.make_async_remote_copy(
            src_ref=here,
            dst_ref=here,
            send_sem=fsend.at[day, off - 1],
            recv_sem=frecv.at[day, off - 1],
            device_id=(sibling, side),
            device_id_type=MESH,
        )

    def direct(day):
        return pltpu.make_async_remote_copy(
            src_ref=spectra.at[day],
            dst_ref=spec_all.at[core, day, mine_rows, :],
            send_sem=dsend.at[day],
            recv_sem=drecv.at[day],
            device_id=(sibling, side),
            device_id_type=MESH,
        )

    mask_copy = pltpu.make_async_remote_copy(
        src_ref=mask_hbm,
        dst_ref=mask.at[core],
        send_sem=dsend.at[days],
        recv_sem=drecv.at[days],
        device_id=(sibling, side),
        device_id_type=MESH,
    )

    for day in range(days):
        if day < AHEAD:
            for off in range(1, halves):
                gather(day, off).start()
        if day == 0:
            mask_copy.start()
        direct(day).start()

    stations = local * halves
    loads[0].wait()
    for end in range(2):
        row = lax.broadcasted_iota(jnp.int32, (stations, 2 * rows), 0)
        hot[...] = (pairs[end : end + 1, :] == row).astype(jnp.float32).T
        for part in range(parts):
            for chip in range(chips):
                first = (2 * chip + core) * (own * parts) + part * own
                pick[end, pl.ds(part * per_part + chip * own, own)] = hot[
                    pl.ds(pl.multiple_of(first, own), own)
                ]
    acc[...] = jnp.zeros_like(acc)
    tail[...] = jnp.zeros_like(tail)
    loads[1].wait()
    mask_copy.wait_recv()
    alive = 0.0
    for owner in range(2):
        seen = [
            lax.dot_general(
                pick[end],
                mask[owner].astype(jnp.float32),
                (((1,), (1,)), ((), ())),
                preferred_element_type=jnp.float32,
            )
            for end in range(2)
        ]
        alive += jnp.sum(seen[0] * seen[1], 1, keepdims=True)
    lane = lax.broadcasted_iota(jnp.int32, (rows, 128), 1)
    count[...] = jnp.where(lane == 96, alive, 0.0)
    turn[...] = (
        (
            lax.broadcasted_iota(jnp.int32, (WIDE, WIDE), 0)
            + lax.broadcasted_iota(jnp.int32, (WIDE, WIDE), 1)
            == MAXLAG
        )
        .astype(jnp.float32)
        .astype(jnp.bfloat16)
    )
    loads[2].wait()
    loads[3].wait()

    def correlate(owner, day, start, size):
        today = mask[owner, pl.ds(day, 1), :].astype(jnp.float32)
        spec = spec_all[owner, day]
        here = pl.ds(start, size)
        both = jnp.dot(
            (pick[:, here] * today).astype(jnp.bfloat16).reshape(2 * size, spec.shape[0]),
            spec,
            preferred_element_type=jnp.float32,
        )
        left_re, left_im = both[:size, :F], both[:size, F:]
        right_re, right_im = both[size:, :F], both[size:, F:]
        cross = jnp.concatenate(
            [
                (left_re * right_re + left_im * right_im).astype(jnp.bfloat16),
                (left_im * right_re - left_re * right_im).astype(jnp.bfloat16),
            ],
            0,
        )
        waves = jnp.dot(cross, table_v[...], preferred_element_type=jnp.float32)
        re_cos, re_sin = waves[:size, :WIDE], waves[:size, WIDE:]
        im_cos, im_sin = waves[size:, :WIDE], waves[size:, WIDE:]
        for back in range(2):
            if back:
                trace, hilbert = re_cos + im_sin, im_cos - re_sin
            else:
                trace, hilbert = re_cos - im_sin, im_cos + re_sin
            inverse = lax.rsqrt(jnp.maximum(trace * trace + hilbert * hilbert, 0.25))
            for n, value in enumerate((trace, trace * inverse, hilbert * inverse)):
                j = 2 * n + back
                acc[here, j * 128 : (j + 1) * 128] += value[:, :128]
                tail[j, here] += value[:, 128:]

    def exchange(s, k):
        part, n, _, _, order = streams[s]
        blocks = chips >> (k + 1)
        base = chips - (chips >> k)
        return pltpu.make_async_remote_copy(
            src_ref=outbox[n].at[part, pl.ds(base, blocks)],
            dst_ref=inbox[n].at[part, pl.ds(base, blocks)],
            send_sem=rsend.at[s, k],
            recv_sem=rrecv.at[s, k],
            device_id=(partner(order[k])[1], side),
            device_id_type=MESH,
        )

    def first_rows(part, order, i, bit):
        natural = sum(((i >> (steps - 1 - n)) & 1) << order[n] for n in range(1, steps))
        first = part * per_part + (natural + bit * (1 << order[0])) * own
        return pl.ds(pl.multiple_of(first, own), own)

    def send(s, k):
        part, n, lane0, width, order = streams[s]
        theirs = 1 - partner(order[k])[0]
        blocks = chips >> (k + 1)
        base = chips - (chips >> k)
        before = chips - (chips >> (k - 1)) if k else 0
        for i in range(blocks):
            if k == 0:
                sent = acc[first_rows(part, order, i, theirs), pl.ds(lane0, width)]
            else:
                sent = work[n][part, before + theirs * blocks + i]
            outbox[n][part, base + i] = sent.astype(jnp.bfloat16)
        exchange(s, k).start()

    def receive(s, k):
        part, n, lane0, width, order = streams[s]
        mine = partner(order[k])[0]
        blocks = chips >> (k + 1)
        base = chips - (chips >> k)
        before = chips - (chips >> (k - 1)) if k else 0
        exchange(s, k).wait_recv()
        for i in range(blocks):
            if k == 0:
                kept = acc[first_rows(part, order, i, mine), pl.ds(lane0, width)]
            else:
                kept = work[n][part, before + mine * blocks + i]
            work[n][part, base + i] = kept + inbox[n][part, base + i].astype(jnp.float32)

    def own_day(day):
        for off in range(1, halves):
            gather(day, off).wait_recv()
            forward(day, off).start()

        @pl.when(day + AHEAD < days)
        def _():
            for off in range(1, halves):
                gather(day + AHEAD, off).start()

        correlate(core, day, 0, rows)
        direct(day).wait_recv()
        for off in range(1, halves):
            forward(day, off).wait_recv()

    def one_day(day, carry):
        own_day(day)
        correlate(1 - core, day, 0, rows)
        return carry

    lax.fori_loop(0, days - 1, one_day, 0)
    own_day(days - 1)
    for part in range(parts):
        here = pl.ds(part * per_part, per_part)
        correlate(1 - core, days - 1, part * per_part, per_part)
        packed = False
        for s in range(len(streams)):
            if streams[s][0] == part:
                if not packed and streams[s][2] + streams[s][3] > 6 * 128:
                    acc[here, 6 * 128 :] = packed_rest([tail[j, here] for j in range(6)], count[here])
                    packed = True
                send(s, 0)

    def finish(part):
        whole = jnp.concatenate([work[n][part, chips - 2] for n in range(len(SHARES))], 1)
        sums, total = unpacked(whole)
        linear = [sums[back] / total for back in range(2)]
        weighted = [
            linear[back]
            * (sums[2 + back] * sums[2 + back] + sums[4 + back] * sums[4 + back])
            / (total * total)
            for back in range(2)
        ]
        ordered = in_order(
            *(jnp.concatenate([linear[back], weighted[back]], 0) for back in range(2)), turn[...]
        )
        here = pl.ds(part * own, own)
        lin_out[here] = ordered[:own]
        wgt_out[here] = ordered[own:]

    for k in range(steps):
        for s in range(len(streams)):
            receive(s, k)
            if k + 1 < steps:
                send(s, k + 1)
            elif s + 1 == len(streams) or streams[s + 1][0] != streams[s][0]:
                finish(streams[s][0])

    mask_copy.wait_send()
    for day in range(days):
        direct(day).wait_send()
        for off in range(1, halves):
            gather(day, off).wait_send()
            forward(day, off).wait_send()
    for s in range(len(streams)):
        for k in range(steps):
            exchange(s, k).wait_send()


def per_device(spectra, pair_list, mask, *, groups, halves):
    days, local, width = spectra.shape
    chips = groups // 2
    rows = pair_list.shape[0] // 2
    parts = parts_of(rows // chips)
    own = rows // chips // parts
    steps = chips.bit_length() - 1
    streams = len(streams_of(steps, parts))
    stations = local * halves
    operands = (spectra, pair_list.T, mask, jnp.asarray(lag_table()))
    hbm = pl.BlockSpec(memory_space=pltpu.HBM)
    vmem = pl.BlockSpec(memory_space=pltpu.VMEM)
    lin, wgt = pl.pallas_call(
        functools.partial(kernel, chips, halves),
        out_shape=[jax.ShapeDtypeStruct((own * parts, LANES), jnp.float32)] * 2,
        in_specs=[hbm] * 4,
        out_specs=[vmem, vmem],
        scratch_shapes=[
            pltpu.VMEM((2, days, stations, width), jnp.bfloat16),
            pltpu.VMEM((F, 2 * WIDE), jnp.bfloat16),
            pltpu.VMEM((2, 2 * rows), jnp.int32),
            pltpu.VMEM((2, *mask.shape), jnp.int32),
            pltpu.VMEM((2 * rows, stations), jnp.float32),
            pltpu.VMEM((2, rows, stations), jnp.float32),
            pltpu.VMEM((rows, PACKED), jnp.float32),
            pltpu.VMEM((6, rows, 128), jnp.float32),
            pltpu.VMEM((rows, 128), jnp.float32),
            pltpu.VMEM((WIDE, WIDE), jnp.bfloat16),
            *(
                pltpu.VMEM((parts, chips, own, share), dtype)
                for dtype in (jnp.float32, jnp.bfloat16, jnp.bfloat16)
                for share in SHARES
            ),
            pltpu.SemaphoreType.DMA((4,)),
            pltpu.SemaphoreType.DMA((days, halves - 1)),
            pltpu.SemaphoreType.DMA((days, halves - 1)),
            pltpu.SemaphoreType.DMA((days, halves - 1)),
            pltpu.SemaphoreType.DMA((days, halves - 1)),
            pltpu.SemaphoreType.DMA((days + 1,)),
            pltpu.SemaphoreType.DMA((days + 1,)),
            pltpu.SemaphoreType.DMA((streams, steps)),
            pltpu.SemaphoreType.DMA((streams, steps)),
        ],
        compiler_params=pltpu.CompilerParams(
            collective_id=0, has_side_effects=True, vmem_limit_bytes=VMEM_LIMIT
        ),
    )(*[pltpu.with_memory_space_constraint(x, pltpu.HBM) for x in operands])
    return lin[:, :LAGS].T, wgt[:, :LAGS].T


def solution(mesh):
    in_specs = (P("day", "pair", None), P("pair", None), P("day", None))
    out_specs = (P(None, ("pair", "day")), P(None, ("pair", "day")))
    return jax.shard_map(
        functools.partial(per_device, groups=mesh.shape["day"], halves=mesh.shape["pair"]),
        mesh=mesh,
        in_specs=in_specs,
        out_specs=out_specs,
        check_vma=False,
    )
```

```python
import functools
import math

import jax
import jax.numpy as jnp
import ml_dtypes
import numpy as np
from jax import lax
from jax.experimental import pallas as pl
from jax.experimental.pallas import tpu as pltpu
from jax.sharding import PartitionSpec as P

F = 512
MAXLAG = 200
LAGS = 401
LANES = 512
WIDE = 256
PACKED = 1280
SHARES = (384, 384, 256, 256)
AHEAD = 4
MESH = pl.DeviceIdType.MESH
VMEM_LIMIT = 40 * 1024 * 1024


def lag_table():
    lag = np.arange(MAXLAG + 1)
    freq = np.arange(F)
    phase = np.mod(lag[None, :] * freq[:, None], 2 * F) * (math.pi / F)
    table = np.zeros((F, 2 * WIDE), np.float32)
    table[:, : MAXLAG + 1] = np.cos(phase) / math.sqrt(F)
    table[:, WIDE : WIDE + MAXLAG + 1] = np.sin(phase) / math.sqrt(F)
    return table.astype(ml_dtypes.bfloat16)


def packed_rest(tail, count):
    lane = lax.broadcasted_iota(jnp.int32, count.shape, 1)
    tiles = [
        jnp.where(lane < 64, tail[2 * n], pltpu.roll(tail[2 * n + 1], 64, 1)) for n in range(3)
    ]
    ends = count
    for j in range(6):
        ends += pltpu.roll(jnp.where(lane >= 64, tail[j], 0.0), (16 * j + 64) % 128, 1)
    return jnp.concatenate(tiles + [ends], 1)


def unpacked(whole):
    tile = [whole[:, n * 128 : (n + 1) * 128] for n in range(PACKED // 128)]
    lane = lax.broadcasted_iota(jnp.int32, tile[0].shape, 1)
    sums = []
    for j in range(6):
        middle = tile[6 + j // 2] if j % 2 == 0 else pltpu.roll(tile[6 + j // 2], 64, 1)
        end = pltpu.roll(tile[9], (192 - 16 * j) % 128, 1)
        rest = jnp.where(lane < 64, middle, jnp.where(lane < 73, end, 0.0))
        sums.append(jnp.concatenate([tile[j], rest], 1))
    return sums, tile[9][:, 96:97]


def in_order(plus, minus, turn):
    rows = minus.shape[0]
    high = minus.astype(jnp.bfloat16)
    left = minus - high.astype(jnp.float32)
    middle = left.astype(jnp.bfloat16)
    low = (left - middle.astype(jnp.float32)).astype(jnp.bfloat16)
    terms = jnp.dot(
        jnp.concatenate([high, middle, low], 0), turn, preferred_element_type=jnp.float32
    )
    turned = terms[:rows] + terms[rows : 2 * rows] + terms[2 * rows :]
    near, far = (pltpu.roll(plus[:, n * 128 : (n + 1) * 128], 72, 1) for n in range(2))
    lane = lax.broadcasted_iota(jnp.int32, near.shape, 1)
    return jnp.concatenate(
        [
            turned[:, :128],
            jnp.where(lane < 72, turned[:, 128:], near),
            jnp.where(lane < 72, near, far),
            far,
        ],
        1,
    )


def parts_of(own):
    return 2 if own % 32 == 0 else 1


def parts_of(own):
    return 2 if own % 32 == 0 else 1


def streams_of(steps, parts):
    straight = list(range(steps))
    swapped = straight[1::-1] + straight[2:]
    return [
        (p, n, sum(SHARES[:n]), SHARES[n], swapped if n % 2 else straight)
        for p in range(parts)
        for n in range(len(SHARES))
    ]


def kernel(
    chips, halves, spectra, pairs_hbm, mask_hbm, table, lin_out, wgt_out,
    spec_all, table_v, pairs, mask, hot, pick, acc, tail, count, turn, *boxes_and_semaphores,
):
    kinds = len(SHARES)
    work, outbox, inbox = (boxes_and_semaphores[kinds * n : kinds * (n + 1)] for n in range(3))
    load_sem, gsend, grecv, fsend, frecv, dsend, drecv, rsend, rrecv = boxes_and_semaphores[3 * kinds :]
    days, local, _ = spectra.shape
    rows = acc.shape[0]
    steps = chips.bit_length() - 1
    parts = parts_of(rows // chips)
    per_part = rows // parts
    own = per_part // chips
    streams = streams_of(steps, parts)
    me = lax.axis_index("day")
    side = lax.axis_index("pair")
    core = lax.rem(me, 2)
    sibling = me + 1 - 2 * core

    def partner(bit):
        size = 2 << bit
        mine = lax.rem(lax.div(me, size), 2)
        return mine, me + (1 - 2 * mine) * size

    def stations_of(where):
        return pl.ds(pl.multiple_of(where * local, local), local)

    mine_rows = stations_of(side)
    loads = [
        pltpu.make_async_copy(pairs_hbm, pairs, load_sem.at[0]),
        pltpu.make_async_copy(mask_hbm, mask.at[core], load_sem.at[1]),
        pltpu.make_async_copy(spectra, spec_all.at[core, :, mine_rows, :], load_sem.at[2]),
        pltpu.make_async_copy(table, table_v, load_sem.at[3]),
    ]
    for copy in loads:
        copy.start()

    barrier = pltpu.get_barrier_semaphore()
    for off in range(1, halves):
        pl.semaphore_signal(
            barrier, inc=1, device_id=(me, lax.rem(side + off, halves)), device_id_type=MESH
        )
    pl.semaphore_signal(barrier, inc=1, device_id=(sibling, side), device_id_type=MESH)
    for bit in range(steps):
        pl.semaphore_signal(barrier, inc=1, device_id=(partner(bit)[1], side), device_id_type=MESH)
    pl.semaphore_wait(barrier, halves + steps)

    def gather(day, off):
        return pltpu.make_async_remote_copy(
            src_ref=spectra.at[day],
            dst_ref=spec_all.at[core, day, mine_rows, :],
            send_sem=gsend.at[day, off - 1],
            recv_sem=grecv.at[day, off - 1],
            device_id=(me, lax.rem(side + off, halves)),
            device_id_type=MESH,
        )

    def forward(day, off):
        here = spec_all.at[core, day, stations_of(lax.rem(side + halves - off, halves)), :]
        return pltpu.make_async_remote_copy(
            src_ref=here,
            dst_ref=here,
            send_sem=fsend.at[day, off - 1],
            recv_sem=frecv.at[day, off - 1],
            device_id=(sibling, side),
            device_id_type=MESH,
        )

    def direct(day):
        return pltpu.make_async_remote_copy(
            src_ref=spectra.at[day],
            dst_ref=spec_all.at[core, day, mine_rows, :],
            send_sem=dsend.at[day],
            recv_sem=drecv.at[day],
            device_id=(sibling, side),
            device_id_type=MESH,
        )

    mask_copy = pltpu.make_async_remote_copy(
        src_ref=mask_hbm,
        dst_ref=mask.at[core],
        send_sem=dsend.at[days],
        recv_sem=drecv.at[days],
        device_id=(sibling, side),
        device_id_type=MESH,
    )

    for day in range(days):
        if day < AHEAD:
            for off in range(1, halves):
                gather(day, off).start()
        if day == 0:
            mask_copy.start()
        direct(day).start()

    stations = local * halves
    loads[0].wait()
    for end in range(2):
        row = lax.broadcasted_iota(jnp.int32, (stations, 2 * rows), 0)
        hot[...] = (pairs[end : end + 1, :] == row).astype(jnp.float32).T
        for part in range(parts):
            for chip in range(chips):
                first = (2 * chip + core) * (own * parts) + part * own
                pick[end, pl.ds(part * per_part + chip * own, own)] = hot[
                    pl.ds(pl.multiple_of(first, own), own)
                ]
    acc[...] = jnp.zeros_like(acc)
    tail[...] = jnp.zeros_like(tail)
    loads[1].wait()
    mask_copy.wait_recv()
    alive = 0.0
    for owner in range(2):
        seen = [
            lax.dot_general(
                pick[end],
                mask[owner].astype(jnp.float32),
                (((1,), (1,)), ((), ())),
                preferred_element_type=jnp.float32,
            )
            for end in range(2)
        ]
        alive += jnp.sum(seen[0] * seen[1], 1, keepdims=True)
    lane = lax.broadcasted_iota(jnp.int32, (rows, 128), 1)
    count[...] = jnp.where(lane == 96, alive, 0.0)
    turn[...] = (
        (
            lax.broadcasted_iota(jnp.int32, (WIDE, WIDE), 0)
            + lax.broadcasted_iota(jnp.int32, (WIDE, WIDE), 1)
            == MAXLAG
        )
        .astype(jnp.float32)
        .astype(jnp.bfloat16)
    )
    loads[2].wait()
    loads[3].wait()

    def correlate(owner, day, start, size):
        today = mask[owner, pl.ds(day, 1), :].astype(jnp.float32)
        spec = spec_all[owner, day]
        here = pl.ds(start, size)
        both = jnp.dot(
            (pick[:, here] * today).astype(jnp.bfloat16).reshape(2 * size, spec.shape[0]),
            spec,
            preferred_element_type=jnp.float32,
        )
        left_re, left_im = both[:size, :F], both[:size, F:]
        right_re, right_im = both[size:, :F], both[size:, F:]
        cross = jnp.concatenate(
            [
                (left_re * right_re + left_im * right_im).astype(jnp.bfloat16),
                (left_im * right_re - left_re * right_im).astype(jnp.bfloat16),
            ],
            0,
        )
        waves = jnp.dot(cross, table_v[...], preferred_element_type=jnp.float32)
        re_cos, re_sin = waves[:size, :WIDE], waves[:size, WIDE:]
        im_cos, im_sin = waves[size:, :WIDE], waves[size:, WIDE:]
        for back in range(2):
            if back:
                trace, hilbert = re_cos + im_sin, im_cos - re_sin
            else:
                trace, hilbert = re_cos - im_sin, im_cos + re_sin
            inverse = lax.rsqrt(jnp.maximum(trace * trace + hilbert * hilbert, 0.25))
            for n, value in enumerate((trace, trace * inverse, hilbert * inverse)):
                j = 2 * n + back
                acc[here, j * 128 : (j + 1) * 128] += value[:, :128]
                tail[j, here] += value[:, 128:]

    def exchange(s, k):
        part, n, _, _, order = streams[s]
        blocks = chips >> (k + 1)
        base = chips - (chips >> k)
        return pltpu.make_async_remote_copy(
            src_ref=outbox[n].at[part, pl.ds(base, blocks)],
            dst_ref=inbox[n].at[part, pl.ds(base, blocks)],
            send_sem=rsend.at[s, k],
            recv_sem=rrecv.at[s, k],
            device_id=(partner(order[k])[1], side),
            device_id_type=MESH,
        )

    def first_rows(part, order, i, bit):
        natural = sum(((i >> (steps - 1 - n)) & 1) << order[n] for n in range(1, steps))
        first = part * per_part + (natural + bit * (1 << order[0])) * own
        return pl.ds(pl.multiple_of(first, own), own)

    def send(s, k):
        part, n, lane0, width, order = streams[s]
        theirs = 1 - partner(order[k])[0]
        blocks = chips >> (k + 1)
        base = chips - (chips >> k)
        before = chips - (chips >> (k - 1)) if k else 0
        for i in range(blocks):
            if k == 0:
                sent = acc[first_rows(part, order, i, theirs), pl.ds(lane0, width)]
            else:
                sent = work[n][part, before + theirs * blocks + i]
            outbox[n][part, base + i] = sent.astype(jnp.bfloat16)
        exchange(s, k).start()

    def receive(s, k):
        part, n, lane0, width, order = streams[s]
        mine = partner(order[k])[0]
        blocks = chips >> (k + 1)
        base = chips - (chips >> k)
        before = chips - (chips >> (k - 1)) if k else 0
        exchange(s, k).wait_recv()
        for i in range(blocks):
            if k == 0:
                kept = acc[first_rows(part, order, i, mine), pl.ds(lane0, width)]
            else:
                kept = work[n][part, before + mine * blocks + i]
            work[n][part, base + i] = kept + inbox[n][part, base + i].astype(jnp.float32)

    def own_day(day):
        for off in range(1, halves):
            gather(day, off).wait_recv()
            forward(day, off).start()

        @pl.when(day + AHEAD < days)
        def _():
            for off in range(1, halves):
                gather(day + AHEAD, off).start()

        correlate(core, day, 0, rows)
        direct(day).wait_recv()
        for off in range(1, halves):
            forward(day, off).wait_recv()

    def one_day(day, carry):
        own_day(day)
        correlate(1 - core, day, 0, rows)
        return carry

    lax.fori_loop(0, days - 1, one_day, 0)
    own_day(days - 1)
    for part in range(parts):
        here = pl.ds(part * per_part, per_part)
        correlate(1 - core, days - 1, part * per_part, per_part)
        packed = False
        for s in range(len(streams)):
            if streams[s][0] == part:
                if not packed and streams[s][2] + streams[s][3] > 6 * 128:
                    acc[here, 6 * 128 :] = packed_rest([tail[j, here] for j in range(6)], count[here])
                    packed = True
                send(s, 0)

    def finish(part):
        whole = jnp.concatenate([work[n][part, chips - 2] for n in range(len(SHARES))], 1)
        sums, total = unpacked(whole)
        linear = [sums[back] / total for back in range(2)]
        weighted = [
            linear[back]
            * (sums[2 + back] * sums[2 + back] + sums[4 + back] * sums[4 + back])
            / (total * total)
            for back in range(2)
        ]
        ordered = in_order(
            *(jnp.concatenate([linear[back], weighted[back]], 0) for back in range(2)), turn[...]
        )
        here = pl.ds(part * own, own)
        lin_out[here] = ordered[:own]
        wgt_out[here] = ordered[own:]

    for k in range(steps):
        for s in range(len(streams)):
            receive(s, k)
            if k + 1 < steps:
                send(s, k + 1)
            elif s + 1 == len(streams) or streams[s + 1][0] != streams[s][0]:
                finish(streams[s][0])

    mask_copy.wait_send()
    for day in range(days):
        direct(day).wait_send()
        for off in range(1, halves):
            gather(day, off).wait_send()
            forward(day, off).wait_send()
    for s in range(len(streams)):
        for k in range(steps):
            exchange(s, k).wait_send()


def per_device(spectra, pair_list, mask, *, groups, halves):
    days, local, width = spectra.shape
    chips = groups // 2
    rows = pair_list.shape[0] // 2
    parts = parts_of(rows // chips)
    own = rows // chips // parts
    steps = chips.bit_length() - 1
    streams = len(streams_of(steps, parts))
    stations = local * halves
    operands = (spectra, pair_list.T, mask, jnp.asarray(lag_table()))
    hbm = pl.BlockSpec(memory_space=pltpu.HBM)
    vmem = pl.BlockSpec(memory_space=pltpu.VMEM)
    lin, wgt = pl.pallas_call(
        functools.partial(kernel, chips, halves),
        out_shape=[jax.ShapeDtypeStruct((own * parts, LANES), jnp.float32)] * 2,
        in_specs=[hbm] * 4,
        out_specs=[vmem, vmem],
        scratch_shapes=[
            pltpu.VMEM((2, days, stations, width), jnp.bfloat16),
            pltpu.VMEM((F, 2 * WIDE), jnp.bfloat16),
            pltpu.VMEM((2, 2 * rows), jnp.int32),
            pltpu.VMEM((2, *mask.shape), jnp.int32),
            pltpu.VMEM((2 * rows, stations), jnp.float32),
            pltpu.VMEM((2, rows, stations), jnp.float32),
            pltpu.VMEM((rows, PACKED), jnp.float32),
            pltpu.VMEM((6, rows, 128), jnp.float32),
            pltpu.VMEM((rows, 128), jnp.float32),
            pltpu.VMEM((WIDE, WIDE), jnp.bfloat16),
            *(
                pltpu.VMEM((parts, chips, own, share), dtype)
                for dtype in (jnp.float32, jnp.bfloat16, jnp.bfloat16)
                for share in SHARES
            ),
            pltpu.SemaphoreType.DMA((4,)),
            pltpu.SemaphoreType.DMA((days, halves - 1)),
            pltpu.SemaphoreType.DMA((days, halves - 1)),
            pltpu.SemaphoreType.DMA((days, halves - 1)),
            pltpu.SemaphoreType.DMA((days, halves - 1)),
            pltpu.SemaphoreType.DMA((days + 1,)),
            pltpu.SemaphoreType.DMA((days + 1,)),
            pltpu.SemaphoreType.DMA((streams, steps)),
            pltpu.SemaphoreType.DMA((streams, steps)),
        ],
        compiler_params=pltpu.CompilerParams(
            collective_id=0, has_side_effects=True, vmem_limit_bytes=VMEM_LIMIT
        ),
    )(*[pltpu.with_memory_space_constraint(x, pltpu.HBM) for x in operands])
    return lin[:, :LAGS].T, wgt[:, :LAGS].T


def solution(mesh):
    in_specs = (P("day", "pair", None), P("pair", None), P("day", None))
    out_specs = (P(None, ("pair", "day")), P(None, ("pair", "day")))
    return jax.shard_map(
        functools.partial(per_device, groups=mesh.shape["day"], halves=mesh.shape["pair"]),
        mesh=mesh,
        in_specs=in_specs,
        out_specs=out_specs,
        check_vma=False,
    )
```
